32 devices in a mesh: slab: 16 (over z, x, core), tile: 2 (over y).
Axes of the slice: x: 2, y: 2, z: 4, core: 2. Of those that a mesh axis runs over, the one named last changes fastest.
Arguments:
- position: float32 [3, 262144], P(None, ('slab', 'tile')), may hold values from 0 to 2.5
- velocity: float32 [3, 262144], P(None, ('slab', 'tile')), may hold values from -6 to 6
- particle_mass: float32 [262144], P(('slab', 'tile')), may hold values from 0.005 to 0.02
- density: float32 [262144], P(('slab', 'tile')), may hold values from 0.8 to 1.25
- deviator: float32 [6, 262144], P(None, ('slab', 'tile')), may hold values from -4 to 4
- plastic: float32 [262144], P(('slab', 'tile')), may hold values from 0.001 to 0.3
- energy: float32 [262144], P(('slab', 'tile')), may hold values from 0.05 to 1
- block_fill: int32 [2048], P(('slab', 'tile')), may hold values from 32 to 128
- pair_blocks: int32 [2, 2048], P(None, ('slab', 'tile')), may hold values from 0 to 127, as said below
- pair_count: int32 [32], P(('slab', 'tile')), may hold values from 8 to 64, as said below
- slab_send: int32 [2, 512], P(None, ('slab', 'tile')), may hold values from 0 to 63
- tile_send: int32 [2, 512], P(None, ('slab', 'tile')), may hold values from 0 to 95
Outputs:
- motion: float32 [4, 262144], P(None, ('slab', 'tile'))
- material: float32 [8, 262144], P(None, ('slab', 'tile'))
The draws below stay inside these ranges and needn't reach their ends.
Inputs may be any that keep to these rules, and one draw needn't show every extreme that they name: `pair_blocks`: row 0 names a block of the device's own 64; row 1 any block of its table of 128: own blocks, then 16 from the lower and 16 from the upper slab neighbour, then 16 from the lower and 16 from the upper tile neighbour. A pair may repeat or name one block twice. `pair_count`: slots from the first up to this count are live, the rest are padding. Loads differ strongly between devices, and some device has all 64 slots live. `block_fill`: the live particles of a block are its first slots. `slab_send`: row 0 lists 16 own blocks for the lower, row 1 for the upper slab neighbour; repeats are allowed. `tile_send`: row 0 lists 16 blocks for the lower, row 1 for the upper tile neighbour, as indices into the extended list of own blocks and received slab blocks; repeats are allowed.
All inputs are finite; a program needn't handle non-finite values.
Results may differ from the reference program's by a relative error of at most 0.0003.
Values sent between devices are 32-bit elements; how exact they have to be, the bound alone decides.
A program may use at most 64 MiB of HBM per device.

```python
import math
import jax
import jax.numpy as jnp
from jax import lax

BLK = 128
NB = 64
GS = 16
PAIRS = 64
PGROUP = 16
SWEEPS = 3
DEVS = 32
PARTICLES = 262144
N_SLAB = 16
N_TILE = 2


def draw_pair_blocks(key, part):
    first_key, second_key = jax.random.split(jax.random.fold_in(key, 11))
    first_rows = jax.random.randint(first_key, (DEVS, PAIRS), 0, NB)
    second_rows = jax.random.randint(second_key, (DEVS, PAIRS), 0, NB + 4 * GS)
    return jnp.stack([first_rows.reshape(-1), second_rows.reshape(-1)]).astype(jnp.int32)


def draw_pair_count(key, part):
    quiet_key, busy_key, pick_key, top_key = jax.random.split(jax.random.fold_in(key, 23), 4)
    quiet_counts = jax.random.randint(quiet_key, (DEVS,), PAIRS // 8, PAIRS // 3 + 1)
    busy_counts = jax.random.randint(busy_key, (DEVS,), 3 * PAIRS // 4, PAIRS + 1)
    ordering = jax.random.permutation(pick_key, DEVS)
    crowded = ordering < max(DEVS // 8, 1)
    counts = jnp.where(crowded, busy_counts, quiet_counts)
    top_device = jax.random.randint(top_key, (), 0, DEVS)
    counts = jnp.where(jnp.arange(DEVS) == top_device, PAIRS, counts)
    return counts.astype(jnp.int32)


def place_ends(drawn, key, low, high):
    spot = [jax.random.randint(jax.random.fold_in(key, axis), (), 0, length) for axis, length in enumerate(drawn.shape)]
    widest = drawn.shape.index(max(drawn.shape))
    next_to = spot[:widest] + [(spot[widest] + 1) % drawn.shape[widest]] + spot[widest + 1:]
    return drawn.at[tuple(spot)].set(low).at[tuple(next_to)].set(high)


def level_of(key, dims, pieces, least, top_value):
    def one(dim, blocks):
        heights = jax.random.uniform(jax.random.fold_in(jax.random.fold_in(key, 6), dim), (blocks,), jnp.float32, least / len(pieces), top_value / len(pieces))
        return jnp.repeat(jnp.exp(heights), dims[dim] // blocks).reshape((-1,) + (1,) * (len(dims) - dim - 1))

    loudness = one(*pieces[0])
    for cut in pieces[1:]:
        loudness = loudness * one(*cut)
    return loudness


def bell_draw(stream_key, extent, scale, limit, cuts=(), held_as=jnp.bfloat16):
    drawn = scale * jax.random.normal(stream_key, extent, jnp.float32)
    if cuts:
        drawn = drawn * level_of(stream_key, extent, cuts, -0.22, 0.18)
    return jnp.clip(drawn, -limit, limit).astype(held_as)


def setup_inputs(seed: int = 0) -> dict:
    arg_keys = jax.random.split(jax.random.key(seed), 13)
    position = jnp.clip(2.5 * jax.random.uniform(arg_keys[0], (3, PARTICLES), jnp.float32) ** level_of(arg_keys[0], (3, PARTICLES), ((1, 32),), -0.2, 0.2), 0.0, 2.5)
    velocity = bell_draw(arg_keys[1], (3, PARTICLES), 1.0, 6.0, ((1, 32),), jnp.float32)
    particle_mass = jnp.clip(jnp.exp(math.log(0.02) - 1.3862944 * jax.random.uniform(arg_keys[2], (PARTICLES,), jnp.float32) ** level_of(arg_keys[2], (PARTICLES,), ((0, 32),), -0.2, 0.2)), 0.005, 0.02)
    density = jnp.clip(jnp.exp(math.log(1.25) - 0.4462871 * jax.random.uniform(arg_keys[3], (PARTICLES,), jnp.float32) ** level_of(arg_keys[3], (PARTICLES,), ((0, 32),), -0.2, 0.2)), 0.8, 1.25)
    deviator = bell_draw(arg_keys[4], (6, PARTICLES), 0.6, 4.0, ((1, 32),), jnp.float32)
    plastic = jnp.clip(jnp.exp(math.log(0.3) - 5.7037825 * jax.random.uniform(arg_keys[5], (PARTICLES,), jnp.float32) ** level_of(arg_keys[5], (PARTICLES,), ((0, 32),), -0.2, 0.2)), 0.001, 0.3)
    energy = jnp.clip(jnp.exp(math.log(1.0) - 2.9957323 * jax.random.uniform(arg_keys[6], (PARTICLES,), jnp.float32) ** level_of(arg_keys[6], (PARTICLES,), ((0, 32),), -0.2, 0.2)), 0.05, 1.0)
    block_fill = place_ends(jax.random.randint(arg_keys[7], (DEVS * NB,), BLK // 4, BLK + 1), jax.random.fold_in(arg_keys[7], 1), BLK // 4, BLK).astype(jnp.int32)
    pair_blocks = draw_pair_blocks(jax.random.fold_in(arg_keys[12], 71), 0)
    pair_count = draw_pair_count(jax.random.fold_in(arg_keys[12], 71), 0)
    slab_send = place_ends(jax.random.randint(arg_keys[10], (2, DEVS * GS), 0, NB), jax.random.fold_in(arg_keys[10], 1), 0, NB - 1).astype(jnp.int32)
    tile_send = place_ends(jax.random.randint(arg_keys[11], (2, DEVS * GS), 0, NB + 2 * GS), jax.random.fold_in(arg_keys[11], 1), 0, (NB + 2 * GS) - 1).astype(jnp.int32)
    return {"position": position, "velocity": velocity, "particle_mass": particle_mass, "density": density, "deviator": deviator, "plastic": plastic, "energy": energy, "block_fill": block_fill, "pair_blocks": pair_blocks, "pair_count": pair_count, "slab_send": slab_send, "tile_send": tile_send}


SMOOTHING = 1.0
KERNEL_SCALE = -105.0 / (16.0 * math.pi)
TIME_STEP = 0.05
SHEAR_MODULUS = 1.0
BULK_MODULUS = 2.0
DENSITY_REF = 1.0
YIELD_BASE = 0.3
HARDEN_COEF = 2.0
HARDEN_EXPONENT = 0.31
RATE_COEF = 0.025
RATE_REF = 0.02
THERMAL_EXPONENT = 1.09
ENERGY_REF = 1.0
VISCOUS_ALPHA = 1.0
VISCOUS_BETA = 2.0
SOFTENING = 0.01
STRESS_FLOOR = 0.1

def sym_matrix(components):
    return [[components[0], components[3], components[5]], [components[3], components[1], components[4]], [components[5], components[4], components[2]]]

def kernel_terms(first_pos, second_pos):
    deltas = [first_pos[:, k, :, None] - second_pos[:, k, None, :] for k in range(3)]
    radius_sq = deltas[0] * deltas[0] + deltas[1] * deltas[1] + deltas[2] * deltas[2]
    spread = jnp.maximum(1.0 - 0.5 * jnp.sqrt(radius_sq) / SMOOTHING, 0.0)
    factor = KERNEL_SCALE * spread * spread * spread
    return (deltas, radius_sq, [factor * one_delta for one_delta in deltas])

def gradient_terms(first_blocks, second_blocks):
    deltas, radius_sq, gradients = kernel_terms(first_blocks[:, 0:3], second_blocks[:, 0:3])
    first_volume = first_blocks[:, 7, :, None]
    second_volume = second_blocks[:, 7, None, :]
    to_first = []
    to_second = []
    for a in range(3):
        vel_diff = second_blocks[:, 3 + a, None, :] - first_blocks[:, 3 + a, :, None]
        for b in range(3):
            product = vel_diff * gradients[b]
            to_first.append(lax.optimization_barrier(jnp.sum(product * second_volume, axis=2)))
            to_second.append(lax.optimization_barrier(jnp.sum(product * first_volume, axis=1)))
    return (jnp.stack(to_first, 1), jnp.stack(to_second, 1))

def force_terms(first_blocks, second_blocks):
    deltas, radius_sq, gradients = kernel_terms(first_blocks[:, 0:3], second_blocks[:, 0:3])
    vel_diff = [first_blocks[:, 3 + k, :, None] - second_blocks[:, 3 + k, None, :] for k in range(3)]
    approach = vel_diff[0] * deltas[0] + vel_diff[1] * deltas[1] + vel_diff[2] * deltas[2]
    closing = SMOOTHING * jnp.minimum(approach, 0.0) / (radius_sq + SOFTENING * SMOOTHING * SMOOTHING)
    mean_sound = 0.5 * (first_blocks[:, 14, :, None] + second_blocks[:, 14, None, :])
    mean_density = 0.5 * (first_blocks[:, 7, :, None] + second_blocks[:, 7, None, :])
    viscous = (-VISCOUS_ALPHA * mean_sound * closing + VISCOUS_BETA * closing * closing) / mean_density
    first_stress = sym_matrix([first_blocks[:, 8 + k, :, None] for k in range(6)])
    second_stress = sym_matrix([second_blocks[:, 8 + k, None, :] for k in range(6)])
    pull_terms = []
    for a in range(3):
        summed = -viscous * gradients[a]
        for b in range(3):
            summed = summed + (first_stress[a][b] + second_stress[a][b]) * gradients[b]
        pull_terms.append(summed)
    heating = -0.5 * (vel_diff[0] * pull_terms[0] + vel_diff[1] * pull_terms[1] + vel_diff[2] * pull_terms[2])
    first_mass = first_blocks[:, 6, :, None]
    second_mass = second_blocks[:, 6, None, :]
    to_first = [lax.optimization_barrier(jnp.sum(second_mass * pull_term, axis=2)) for pull_term in pull_terms]
    to_first.append(lax.optimization_barrier(jnp.sum(second_mass * heating, axis=2)))
    to_second = [-lax.optimization_barrier(jnp.sum(first_mass * pull_term, axis=1)) for pull_term in pull_terms]
    to_second.append(lax.optimization_barrier(jnp.sum(first_mass * heating, axis=1)))
    return (jnp.stack(to_first, 1), jnp.stack(to_second, 1))

def pair_pass(table_blocks, first_ids, second_ids, pair_live, term_fn, term_width):

    def one_group(summed, group_index):
        start_row = group_index * PGROUP
        first_rows = lax.dynamic_slice_in_dim(first_ids, start_row, PGROUP)
        second_rows = lax.dynamic_slice_in_dim(second_ids, start_row, PGROUP)
        weights = lax.dynamic_slice_in_dim(pair_live, start_row, PGROUP)
        to_first, to_second = term_fn(table_blocks[first_rows], table_blocks[second_rows])
        mirror = weights * (first_rows != second_rows).astype(jnp.float32)
        summed = summed.at[first_rows].add(to_first * weights[:, None, None])
        summed = summed.at[second_rows].add(to_second * mirror[:, None, None])
        return (summed, None)
    zero_sums = jnp.zeros((table_blocks.shape[0], term_width, table_blocks.shape[2]), jnp.float32)
    summed, ignored = lax.scan(one_group, zero_sums, jnp.arange(PAIRS // PGROUP, dtype=jnp.int32))
    return summed

def update_material(velocity_grad, deviator, plastic, energy, density):
    gradient_rows = [[velocity_grad[3 * a + b] for b in range(3)] for a in range(3)]
    strain = [[0.5 * (gradient_rows[a][b] + gradient_rows[b][a]) for b in range(3)] for a in range(3)]
    rotation = [[0.5 * (gradient_rows[a][b] - gradient_rows[b][a]) for b in range(3)] for a in range(3)]
    trace_rate = strain[0][0] + strain[1][1] + strain[2][2]
    new_density = density * jnp.exp(-TIME_STEP * trace_rate)
    mean_normal = (deviator[0] + deviator[1] + deviator[2]) / 3.0
    previous = sym_matrix([deviator[0] - mean_normal, deviator[1] - mean_normal, deviator[2] - mean_normal, deviator[3], deviator[4], deviator[5]])
    shear_rate = [[strain[a][b] - trace_rate / 3.0 if a == b else strain[a][b] for b in range(3)] for a in range(3)]
    trial_stress = []
    for a in range(3):
        trial_row = []
        for b in range(3):
            rate_term = 2.0 * SHEAR_MODULUS * shear_rate[a][b]
            for k in range(3):
                rate_term = rate_term + rotation[a][k] * previous[k][b] - previous[a][k] * rotation[k][b]
            trial_row.append(previous[a][b] + TIME_STEP * rate_term)
        trial_stress.append(trial_row)
    trial_parts = [trial_stress[0][0], trial_stress[1][1], trial_stress[2][2], trial_stress[0][1], trial_stress[1][2], trial_stress[2][0]]
    contract = trial_parts[0] * trial_parts[0] + trial_parts[1] * trial_parts[1] + trial_parts[2] * trial_parts[2] + 2.0 * (trial_parts[3] * trial_parts[3] + trial_parts[4] * trial_parts[4] + trial_parts[5] * trial_parts[5])
    equivalent = jnp.sqrt(1.5 * contract)
    rate_square = shear_rate[0][0] * shear_rate[0][0]
    for a in range(3):
        for b in range(3):
            if a + b > 0:
                rate_square = rate_square + shear_rate[a][b] * shear_rate[a][b]
    rate_equiv = jnp.sqrt(2.0 / 3.0 * rate_square)
    rate_factor = 1.0 + RATE_COEF * jnp.log(jnp.maximum(rate_equiv / RATE_REF, 1.0))
    homologous = energy / (energy + ENERGY_REF)
    scale_now = rate_factor * (1.0 - homologous ** THERMAL_EXPONENT)
    tangent = 3.0 * SHEAR_MODULUS + HARDEN_COEF * HARDEN_EXPONENT * plastic ** (HARDEN_EXPONENT - 1.0) * scale_now
    increment = jnp.zeros_like(plastic)
    for sweep_index in range(SWEEPS):
        flow_stress = (YIELD_BASE + HARDEN_COEF * (plastic + increment) ** HARDEN_EXPONENT) * scale_now
        increment = jnp.maximum(increment + (equivalent - 3.0 * SHEAR_MODULUS * increment - flow_stress) / tangent, 0.0)
    shrink = 1.0 - 3.0 * SHEAR_MODULUS * increment / jnp.maximum(equivalent, STRESS_FLOOR)
    new_deviator = [component * shrink for component in trial_parts]
    pressure = BULK_MODULUS * (new_density / DENSITY_REF - 1.0)
    inverse_sq = 1.0 / (new_density * new_density)
    scaled = [(new_deviator[k] - pressure) * inverse_sq if k < 3 else new_deviator[k] * inverse_sq for k in range(6)]
    sound_speed = jnp.sqrt((BULK_MODULUS + 4.0 / 3.0 * SHEAR_MODULUS) / new_density)
    return (new_deviator, plastic + increment, new_density, scaled, sound_speed)

def as_grid(fields):
    return fields.reshape(fields.shape[0], N_SLAB, N_TILE, NB, BLK).transpose(1, 2, 3, 0, 4)

def from_grid(device_grid):
    return device_grid.transpose(3, 0, 1, 2, 4).reshape(device_grid.shape[3], -1)

def take_rows(device_grid, row_ids):
    return jnp.take_along_axis(device_grid, row_ids[:, :, :, None, None], axis=2)

def shift_grid(device_grid, grid_axis, upward):
    size_along = device_grid.shape[grid_axis]
    border = jnp.zeros_like(lax.slice_in_dim(device_grid, 0, 1, axis=grid_axis))
    if upward:
        return jnp.concatenate([border, lax.slice_in_dim(device_grid, 0, size_along - 1, axis=grid_axis)], grid_axis)
    return jnp.concatenate([lax.slice_in_dim(device_grid, 1, size_along, axis=grid_axis), border], grid_axis)

def build_table(own_grid, slab_rows, tile_rows):
    downward_out = take_rows(own_grid, slab_rows[0])
    upward_out = take_rows(own_grid, slab_rows[1])
    widened = jnp.concatenate([own_grid, shift_grid(upward_out, 0, True), shift_grid(downward_out, 0, False)], 2)
    downward_out = take_rows(widened, tile_rows[0])
    upward_out = take_rows(widened, tile_rows[1])
    return jnp.concatenate([widened, shift_grid(upward_out, 1, True), shift_grid(downward_out, 1, False)], 2)

def add_rows(device_grid, row_ids, additions):

    def add_one(blocks, indices, additions_one):
        return blocks.at[indices].add(additions_one)
    flattened = jax.vmap(add_one)(device_grid.reshape((-1,) + device_grid.shape[2:]), row_ids.reshape(-1, row_ids.shape[2]), additions.reshape((-1,) + additions.shape[2:]))
    return flattened.reshape(device_grid.shape)

def return_table(summed, slab_rows, tile_rows):
    inner_end = NB + 2 * GS
    lower_slots = summed[:, :, inner_end:inner_end + GS]
    upper_slots = summed[:, :, inner_end + GS:]
    widened = summed[:, :, :inner_end]
    widened = add_rows(widened, tile_rows[0], shift_grid(upper_slots, 1, True))
    widened = add_rows(widened, tile_rows[1], shift_grid(lower_slots, 1, False))
    lower_slots = widened[:, :, NB:NB + GS]
    upper_slots = widened[:, :, NB + GS:]
    own_blocks = widened[:, :, :NB]
    own_blocks = add_rows(own_blocks, slab_rows[0], shift_grid(upper_slots, 0, True))
    own_blocks = add_rows(own_blocks, slab_rows[1], shift_grid(lower_slots, 0, False))
    return own_blocks

def device_pass(table_grid, pair_blocks, pair_count, term_fn, term_width):
    flat_table = table_grid.reshape((N_SLAB * N_TILE,) + table_grid.shape[2:])
    firsts = pair_blocks[0].reshape(-1, PAIRS)
    seconds = pair_blocks[1].reshape(-1, PAIRS)

    def one_device(packed):
        table_blocks, first_ids, second_ids, live_count = packed
        pair_live = (jnp.arange(PAIRS, dtype=jnp.int32) < live_count).astype(jnp.float32)
        return pair_pass(table_blocks, first_ids, second_ids, pair_live, term_fn, term_width)
    summed = lax.map(one_device, (flat_table, firsts, seconds, pair_count))
    return summed.reshape(table_grid.shape[:3] + summed.shape[2:])

def reference(position, velocity, particle_mass, density, deviator, plastic, energy, block_fill, pair_blocks, pair_count, slab_send, tile_send):
    slot_index = lax.broadcasted_iota(jnp.int32, (N_SLAB * N_TILE * NB, BLK), 1)
    alive_mask = (slot_index < block_fill[:, None]).astype(jnp.float32).reshape(-1)
    live_mass = particle_mass * alive_mask
    volume = live_mass / density
    slab_rows = slab_send.reshape(2, N_SLAB, N_TILE, GS)
    tile_rows = tile_send.reshape(2, N_SLAB, N_TILE, GS)
    first_fields = jnp.concatenate([position, velocity, live_mass[None], volume[None]], 0)
    table_one = build_table(as_grid(first_fields), slab_rows, tile_rows)
    summed = device_pass(table_one, pair_blocks, pair_count, gradient_terms, 9)
    velocity_grad = from_grid(return_table(summed, slab_rows, tile_rows))
    new_deviator, new_plastic, new_density, scaled, sound_speed = update_material(velocity_grad, deviator, plastic, energy, density)
    second_fields = jnp.concatenate([position, velocity, live_mass[None], new_density[None], jnp.stack(scaled), sound_speed[None]], 0)
    table_two = build_table(as_grid(second_fields), slab_rows, tile_rows)
    summed = device_pass(table_two, pair_blocks, pair_count, force_terms, 4)
    motion = from_grid(return_table(summed, slab_rows, tile_rows))
    material = jnp.concatenate([jnp.stack(new_deviator), new_plastic[None], new_density[None]], 0)
    return (motion, material)
```

```python
import functools
import math

import jax
import jax.numpy as jnp
from jax import lax
from jax.experimental import pallas as pl
from jax.experimental.pallas import tpu as pltpu
from jax.sharding import PartitionSpec as P

MESH = pl.DeviceIdType.MESH
F32 = jnp.float32
BF16 = jnp.bfloat16
SWEEPS = 3
UNROLL = 4
ROWS = 8
R1 = 5 * ROWS
R2 = 9 * ROWS


SMOOTHING = 1.0
KERNEL_SCALE = -105.0 / (16.0 * math.pi)
TIME_STEP = 0.05
SHEAR_MODULUS = 1.0
BULK_MODULUS = 2.0
DENSITY_REF = 1.0
YIELD_BASE = 0.3
HARDEN_COEF = 2.0
HARDEN_EXPONENT = 0.31
RATE_COEF = 0.025
RATE_REF = 0.02
THERMAL_EXPONENT = 1.09
ENERGY_REF = 1.0
VISCOUS_ALPHA = 1.0
VISCOUS_BETA = 2.0
SOFTENING = 0.01
STRESS_FLOOR = 0.1


def power(base, exponent):
    return jnp.exp(exponent * jnp.log(base))


def sym_matrix(components):
    return [
        [components[0], components[3], components[5]],
        [components[3], components[1], components[4]],
        [components[5], components[4], components[2]],
    ]


def update_material(velocity_grad, deviator, plastic, energy, density):
    gradient_rows = [[velocity_grad[3 * a + b] for b in range(3)] for a in range(3)]
    strain = [
        [0.5 * (gradient_rows[a][b] + gradient_rows[b][a]) for b in range(3)] for a in range(3)
    ]
    rotation = [
        [0.5 * (gradient_rows[a][b] - gradient_rows[b][a]) for b in range(3)] for a in range(3)
    ]
    trace_rate = strain[0][0] + strain[1][1] + strain[2][2]
    new_density = density * jnp.exp(-TIME_STEP * trace_rate)
    mean_normal = (deviator[0] + deviator[1] + deviator[2]) / 3.0
    previous = sym_matrix(
        [
            deviator[0] - mean_normal,
            deviator[1] - mean_normal,
            deviator[2] - mean_normal,
            deviator[3],
            deviator[4],
            deviator[5],
        ]
    )
    shear_rate = [
        [strain[a][b] - trace_rate / 3.0 if a == b else strain[a][b] for b in range(3)]
        for a in range(3)
    ]
    trial_stress = []
    for a in range(3):
        trial_row = []
        for b in range(3):
            rate_term = 2.0 * SHEAR_MODULUS * shear_rate[a][b]
            for k in range(3):
                rate_term = (
                    rate_term + rotation[a][k] * previous[k][b] - previous[a][k] * rotation[k][b]
                )
            trial_row.append(previous[a][b] + TIME_STEP * rate_term)
        trial_stress.append(trial_row)
    trial_parts = [
        trial_stress[0][0],
        trial_stress[1][1],
        trial_stress[2][2],
        trial_stress[0][1],
        trial_stress[1][2],
        trial_stress[2][0],
    ]
    contract = (
        trial_parts[0] * trial_parts[0]
        + trial_parts[1] * trial_parts[1]
        + trial_parts[2] * trial_parts[2]
        + 2.0
        * (
            trial_parts[3] * trial_parts[3]
            + trial_parts[4] * trial_parts[4]
            + trial_parts[5] * trial_parts[5]
        )
    )
    equivalent = jnp.sqrt(1.5 * contract)
    rate_square = shear_rate[0][0] * shear_rate[0][0]
    for a in range(3):
        for b in range(3):
            if a + b > 0:
                rate_square = rate_square + shear_rate[a][b] * shear_rate[a][b]
    rate_equiv = jnp.sqrt(2.0 / 3.0 * rate_square)
    rate_factor = 1.0 + RATE_COEF * jnp.log(jnp.maximum(rate_equiv / RATE_REF, 1.0))
    homologous = energy / (energy + ENERGY_REF)
    scale_now = rate_factor * (1.0 - power(homologous, THERMAL_EXPONENT))
    tangent = (
        3.0 * SHEAR_MODULUS
        + HARDEN_COEF * HARDEN_EXPONENT * power(plastic, HARDEN_EXPONENT - 1.0) * scale_now
    )
    increment = jnp.zeros_like(plastic)
    for sweep_index in range(SWEEPS):
        flow_stress = (
            YIELD_BASE + HARDEN_COEF * power(plastic + increment, HARDEN_EXPONENT)
        ) * scale_now
        increment = jnp.maximum(
            increment + (equivalent - 3.0 * SHEAR_MODULUS * increment - flow_stress) / tangent, 0.0
        )
    shrink = 1.0 - 3.0 * SHEAR_MODULUS * increment / jnp.maximum(equivalent, STRESS_FLOOR)
    new_deviator = [component * shrink for component in trial_parts]
    pressure = BULK_MODULUS * (new_density / DENSITY_REF - 1.0)
    inverse_sq = 1.0 / (new_density * new_density)
    scaled = [
        (new_deviator[k] - pressure) * inverse_sq if k < 3 else new_deviator[k] * inverse_sq
        for k in range(6)
    ]
    sound_speed = jnp.sqrt((BULK_MODULUS + 4.0 / 3.0 * SHEAR_MODULUS) / new_density)
    return (new_deviator, plastic + increment, new_density, scaled, sound_speed)


def split_two(value):
    high = value.astype(BF16)
    return (high, (value - high.astype(F32)).astype(BF16))


def split_three(value):
    one = value.astype(BF16).astype(F32)
    rest = value - one
    two = rest.astype(BF16).astype(F32)
    return (one, two, rest - two)


def dot(left, right, contract=(1, 0)):
    return lax.dot_general(
        left, right, (((contract[0],), (contract[1],)), ((), ())), preferred_element_type=F32
    )


def reciprocal(value):
    guess = pl.reciprocal(value, approx=True)
    return guess * (2.0 - value * guess)


def sum_groups(row, first_value, second_value):
    f, s = split_three(first_value), split_three(second_value)
    left = jnp.where(row < 6, 1.0, 0.0)
    right = left
    for k in range(3):
        left = jnp.where(row == k, f[k], left)
        right = jnp.where(row == 3 + k, s[k], right)
    return left, right


def xyz_dot(row, left, right):
    return jnp.sum(jnp.where(row < 3, left * right, 0.0), axis=0, keepdims=True)


def swap(row, tile):
    return jnp.where(row < 3, pltpu.roll(tile, 5, 0), pltpu.roll(tile, 3, 0))


def centred(row, tile, centre):
    moved = jnp.where(row < 6, tile - centre, 1.0)
    along = xyz_dot(row, moved, swap(row, moved))
    return jnp.where(row == 7, along, moved), along


def geometry(row, first, second, first_along, second_along):
    a1, a2, a3 = split_three(first)
    b1, b2, b3 = split_three(second)
    order = (b1, b2, b1, b2, b3, b1)
    near = jnp.where(row < 3, -2.0, 0.0)
    cross = jnp.where(row < 6, -1.0, 0.0)
    swapped = [swap(row, b) * cross for b in (b1, b2, b3)]
    swapped = (swapped[0], swapped[1], swapped[0], swapped[1], swapped[2], swapped[0])
    norm_left, norm_right = sum_groups(
        row, xyz_dot(row, first, first), xyz_dot(row, second, second)
    )
    along_left, along_right = sum_groups(row, first_along, second_along)
    zero = jnp.zeros_like(first)
    left = jnp.concatenate([a1, a1, a2, a2, a1, a3, norm_left, along_left], 0).astype(BF16)
    right_one = jnp.concatenate([b * near for b in order] + [norm_right, zero], 0)
    right_two = jnp.concatenate(list(swapped) + [zero, along_right], 0)
    right = jnp.concatenate([right_one, right_two], 1).astype(BF16)
    both = dot(left, right, (0, 0))
    width = first.shape[1]
    return both[:, :width], both[:, width:]


def weigh(columns, high, low, side):
    count = columns.shape[0]
    top, rest = split_two(columns)
    both = dot(jnp.concatenate([top, rest], 0), high, side)
    return both[:count] + both[count:] + dot(top, low, side)


def gradient_columns(tile, moved):
    volume = tile[7:8]
    base = moved * volume
    return jnp.concatenate([base] + [base * moved[3 + a : 4 + a] for a in range(3)], 0)


def force_columns(row, tile, moved, stress):
    mass = tile[6:7]
    base = moved * mass
    cols = sym_matrix([stress[1 + k : 2 + k] for k in range(6)])
    turned = jnp.zeros_like(moved)
    first_row = jnp.logical_or(row == 0, row == 3)
    second_row = jnp.logical_or(row == 1, row == 4)
    for b in range(3):
        column = jnp.where(first_row, cols[0][b], jnp.where(second_row, cols[1][b], cols[2][b]))
        turned = turned + column * jnp.where(row < 3, moved[b : b + 1], moved[3 + b : 4 + b])
    inner = jnp.zeros_like(mass)
    for a in range(3):
        inner = inner + moved[a : a + 1] * turned[3 + a : 4 + a]
    turned = jnp.where(row < 6, turned, inner)
    return jnp.concatenate(
        [base]
        + [base * moved[3 + a : 4 + a] for a in range(3)]
        + [stress * mass, turned * mass],
        0,
    )


def hot(ids, rows):
    where = lax.broadcasted_iota(jnp.int32, (rows, ids.shape[1]), 0)
    return jnp.where(where == ids, 1.0, 0.0).astype(BF16)


def place(one_hot, value):
    high, low = split_two(value)
    return dot(one_hot, high) + dot(one_hot, low)


class Exchange:
    def __init__(self, axis, size, stage, sends, lands, send_sem, recv_sem):
        self.me = lax.axis_index(axis)
        self.size = size
        self.lands = lands
        self.copies = [
            pltpu.make_async_remote_copy(
                src_ref=sends[d],
                dst_ref=lands[d],
                send_sem=send_sem.at[stage, d],
                recv_sem=recv_sem.at[stage, d],
                device_id={axis: self.me + (1, -1)[d]},
                device_id_type=MESH,
            )
            for d in range(2)
        ]

    def start(self):
        low, high = self.me > 0, self.me < self.size - 1
        pl.when(high)(self.copies[0].start)
        pl.when(low)(self.copies[1].start)

        @pl.when(jnp.logical_not(low))
        def _():
            self.lands[0][...] = jnp.zeros(self.lands[0].shape, F32)

        @pl.when(jnp.logical_not(high))
        def _():
            self.lands[1][...] = jnp.zeros(self.lands[1].shape, F32)

    def wait(self):
        low, high = self.me > 0, self.me < self.size - 1
        pl.when(low)(self.copies[0].wait_recv)
        pl.when(high)(self.copies[1].wait_recv)

    def finish(self):
        low, high = self.me > 0, self.me < self.size - 1
        pl.when(high)(self.copies[0].wait_send)
        pl.when(low)(self.copies[1].wait_send)


def step_kernel(
    sizes,
    pairs_ref,
    slab_ref,
    tile_ref,
    ids_ref,
    position,
    velocity,
    live_mass,
    density,
    deviator,
    plastic,
    energy,
    motion,
    material,
    own_rows,
    table,
    stress_table,
    outgoing,
    arrived,
    slots,
    sums,
    sums_arrived,
    pulls,
    pulls_arrived,
    near_high,
    near_low,
    closing_ref,
    send_sem,
    recv_sem,
):
    n_slab, n_tile, nb, gs, pairs = sizes
    blk = live_mass.shape[1]
    ext = nb + 2 * gs
    full = ext + 2 * gs
    axes = (("slab", n_slab), ("tile", n_tile))

    barrier = pltpu.get_barrier_semaphore()
    expected = 0
    for axis, size in axes:
        me = lax.axis_index(axis)
        for shift, there in ((1, me < size - 1), (-1, me > 0)):

            @pl.when(there)
            def _(axis=axis, me=me, shift=shift):
                pl.semaphore_signal(
                    barrier, inc=1, device_id={axis: me + shift}, device_id_type=MESH
                )

            expected = expected + there.astype(jnp.int32)

    def put(field, value):
        own_rows[pl.ds(field, nb, stride=ROWS), :] = value

    def put_own(ref):
        ref[:nb] = own_rows[...].reshape(nb, ROWS, blk)

    for k in range(3):
        put(k, position[k])
        put(3 + k, velocity[k])
    put(6, live_mass[...])
    put(7, live_mass[...] / density[...])

    def spread(ref, stage, before=None):
        for step, (axis, size) in enumerate(axes):
            ids = (slab_ref, tile_ref)[step]
            at = stage + step
            mine = 2 * (stage // 4) + step
            for d in range(2):
                for k in range(gs):
                    outgoing[mine, d, k] = ref[ids[1 - d, k]]
            if before is not None and step == 0:
                before()
            swapping = Exchange(
                axis,
                size,
                at,
                [outgoing.at[mine, d] for d in range(2)],
                [arrived.at[mine, d] for d in range(2)],
                send_sem,
                recv_sem,
            )
            swapping.start()
            swapping.wait()
            base = (nb, ext)[step]
            for d in range(2):
                ref[base + d * gs : base + (d + 1) * gs] = arrived[mine, d]
            swapping.finish()

    put_own(table)
    spread(table, 0, before=lambda: pl.semaphore_wait(barrier, expected))

    row = lax.broadcasted_iota(jnp.int32, (ROWS, blk), 0)

    def tiles(ref, p):
        return ref[pairs_ref[0, p]], ref[pairs_ref[1, p]]

    def moved_tiles(p):
        first, second = tiles(table, p)
        centre = jnp.mean(first, axis=1, keepdims=True)
        one, one_along = centred(row, first, centre)
        two, two_along = centred(row, second, centre)
        return first, second, one, two, one_along, two_along

    def keep(slot, width, value):
        slots[pl.ds(pl.multiple_of(slot * width, ROWS), width), :] = value

    def gradient_pair(p):
        first, second, one, two, one_along, two_along = moved_tiles(p)
        radius_sq, approach = geometry(row, one, two, one_along, two_along)
        radius_sq = jnp.maximum(radius_sq, 1e-30)
        spread_now = jnp.maximum(1.0 - 0.5 * (radius_sq * lax.rsqrt(radius_sq)), 0.0)
        high, low = split_two(spread_now * spread_now * spread_now)
        near_high[p] = high
        near_low[p] = low
        closing_ref[p] = jnp.minimum(approach, 0.0) * reciprocal(radius_sq + SOFTENING)
        to_first = weigh(gradient_columns(second, two), high, low, (1, 1))
        to_second = weigh(gradient_columns(first, one), high, low, (1, 0))
        keep(p, R1, jnp.concatenate([to_first, one], 0))
        keep(pairs + p, R1, jnp.concatenate([to_second, two], 0))

    def force_pair(p):
        first, second, one, two, one_along, two_along = moved_tiles(p)
        first_stress, second_stress = tiles(stress_table, p)
        sound_left, sound_right = sum_groups(row, first_stress[7:8], second_stress[7:8])
        rho_left, rho_right = sum_groups(row, first_stress[0:1], second_stress[0:1])
        zero = jnp.zeros_like(row, F32)
        right_one = jnp.concatenate([sound_right, zero], 0)
        right_two = jnp.concatenate([zero, rho_right], 0)
        totals = dot(
            jnp.concatenate([sound_left, rho_left], 0).astype(BF16),
            jnp.concatenate([right_one, right_two], 1).astype(BF16),
            (0, 0),
        )
        sound, rho = totals[:, :blk], totals[:, blk:]
        high, low = near_high[p], near_low[p]
        near = high.astype(F32) + low.astype(F32)
        closing = closing_ref[p]
        viscous = near * closing * (4.0 * closing - sound) * reciprocal(rho)
        drag_high, drag_low = split_two(viscous)
        from_second = force_columns(row, second, two, second_stress)
        from_first = force_columns(row, first, one, first_stress)
        keep(
            p,
            R2,
            jnp.concatenate(
                [
                    weigh(from_second, high, low, (1, 1)),
                    weigh(from_second[:ROWS], drag_high, drag_low, (1, 1)),
                    one,
                    first_stress,
                ],
                0,
            ),
        )
        keep(
            pairs + p,
            R2,
            jnp.concatenate(
                [
                    weigh(from_first, high, low, (1, 0)),
                    weigh(from_first[:ROWS], drag_high, drag_low, (1, 0)),
                    two,
                    second_stress,
                ],
                0,
            ),
        )

    def all_pairs(one_pair):
        def some(step, carry):
            for k in range(UNROLL):
                one_pair(step * UNROLL + k)
            return carry

        lax.fori_loop(0, pairs // UNROLL, some, 0)
        for p in range(pairs // UNROLL * UNROLL, pairs):
            one_pair(p)

    pair_hot = hot(ids_ref[0:1, : 2 * pairs], full)
    tile_hot = hot(ids_ref[1:2, : 2 * gs], ext)
    slab_hot = hot(ids_ref[2:3, : 2 * gs], nb)

    def give_back(ref, landing, stage):
        width = ref.shape[0]
        for step, (axis, size) in ((1, axes[1]), (0, axes[0])):
            base = (nb, ext)[step]
            one_hot = (slab_hot, tile_hot)[step]
            at = stage + 1 - step
            swapping = Exchange(
                axis,
                size,
                at,
                [ref.at[:, pl.ds(base + gs, gs), :], ref.at[:, pl.ds(base, gs), :]],
                [landing.at[step, d] for d in range(2)],
                send_sem,
                recv_sem,
            )
            swapping.start()
            swapping.wait()
            for c in range(width):
                come = jnp.concatenate([landing[step, 0, c], landing[step, 1, c]], 0)
                ref[c, :base, :] = ref[c, :base, :] + place(one_hot, come)
            swapping.finish()

    all_pairs(gradient_pair)

    def slot_rows(r, width):
        return slots[pl.ds(r, 2 * pairs, stride=width), :]

    for a in range(3):
        speed = slot_rows(4 * ROWS + 3 + a, R1)
        plain = slot_rows((a + 1) * ROWS + 6, R1) - speed * slot_rows(6, R1)
        for b in range(3):
            bent = slot_rows((a + 1) * ROWS + b, R1) - speed * slot_rows(b, R1)
            sums[3 * a + b] = place(pair_hot, slot_rows(4 * ROWS + b, R1) * plain - bent)
    give_back(sums, sums_arrived, 2)

    velocity_grad = [sums[c, :nb, :] * KERNEL_SCALE for c in range(9)]
    new_deviator, new_plastic, new_density, scaled, sound_speed = update_material(
        velocity_grad, [deviator[k] for k in range(6)], plastic[...], energy[...], density[...]
    )
    for k in range(6):
        material[k] = new_deviator[k]
        put(1 + k, scaled[k])
    material[6] = new_plastic
    material[7] = new_density
    put(0, new_density)
    put(7, sound_speed)
    put_own(stress_table)
    spread(stress_table, 4)

    all_pairs(force_pair)

    def get(r):
        return slot_rows(r, R2)

    place_of = [get(7 * ROWS + k) for k in range(3)]
    own = sym_matrix([get(8 * ROWS + 1 + k) for k in range(6)])
    other = sym_matrix([get(4 * ROWS + 1 + k) for k in range(6)])
    weight = get(6)
    drag = get(6 * ROWS + 6)
    heat = jnp.zeros_like(weight)
    bent = [place_of[b] * weight - get(b) for b in range(3)]
    for a in range(3):
        speed = get(7 * ROWS + 3 + a)
        carried = get(3 + a)
        pull = get(6 * ROWS + a) - place_of[a] * drag - get(5 * ROWS + a)
        inner = place_of[a] * (get(5 * ROWS + 3 + a) - get(6 * ROWS + 3 + a))
        for b in range(3):
            pull = pull + own[a][b] * bent[b] + other[a][b] * place_of[b]
            inner = inner + own[a][b] * (place_of[b] * carried - get((a + 1) * ROWS + b))
        heat = heat + speed * pull - inner
        pulls[a] = place(pair_hot, pull)
    heat = heat + get(5 * ROWS + 6) - get(6 * ROWS + 7)
    pulls[3] = place(pair_hot, heat)
    give_back(pulls, pulls_arrived, 6)
    for k in range(3):
        motion[k] = pulls[k, :nb, :] * KERNEL_SCALE
    motion[3] = pulls[3, :nb, :] * (-0.5 * KERNEL_SCALE)


def body(
    sizes,
    position,
    velocity,
    particle_mass,
    density,
    deviator,
    plastic,
    energy,
    block_fill,
    pair_blocks,
    pair_count,
    slab_send,
    tile_send,
):
    n_slab, n_tile = sizes
    nb = block_fill.shape[0]
    blk = position.shape[1] // nb
    gs = slab_send.shape[1]
    pairs = pair_blocks.shape[1]
    full = nb + 4 * gs
    alive = lax.broadcasted_iota(jnp.int32, (nb, blk), 1) < block_fill[:, None]
    live_mass = jnp.where(alive, particle_mass.reshape(nb, blk), 0.0)
    first, second = pair_blocks[0], pair_blocks[1]
    live = jnp.arange(pairs, dtype=jnp.int32) < pair_count[0]
    lane = max(2 * pairs, 2 * gs)

    def line(values):
        return jnp.pad(values, (0, lane - values.shape[0]), constant_values=-1)

    ids = jnp.stack(
        [
            line(
                jnp.concatenate(
                    [
                        jnp.where(live, first, -1),
                        jnp.where(live & (first != second), second, -1),
                    ]
                )
            ),
            line(tile_send.reshape(-1)),
            line(slab_send.reshape(-1)),
        ]
    )
    smem = pl.BlockSpec(memory_space=pltpu.SMEM)
    vmem = pl.BlockSpec(memory_space=pltpu.VMEM)
    motion, material = pl.pallas_call(
        functools.partial(step_kernel, (n_slab, n_tile, nb, gs, pairs)),
        out_shape=(
            jax.ShapeDtypeStruct((4, nb, blk), F32),
            jax.ShapeDtypeStruct((8, nb, blk), F32),
        ),
        in_specs=[smem] * 3 + [vmem] * 8,
        out_specs=(vmem, vmem),
        scratch_shapes=[
            pltpu.VMEM((nb * ROWS, blk), F32),
            pltpu.VMEM((full, ROWS, blk), F32),
            pltpu.VMEM((full, ROWS, blk), F32),
            pltpu.VMEM((4, 2, gs, ROWS, blk), F32),
            pltpu.VMEM((4, 2, gs, ROWS, blk), F32),
            pltpu.VMEM((2 * pairs * R2, blk), F32),
            pltpu.VMEM((9, full, blk), F32),
            pltpu.VMEM((2, 2, 9, gs, blk), F32),
            pltpu.VMEM((4, full, blk), F32),
            pltpu.VMEM((2, 2, 4, gs, blk), F32),
            pltpu.VMEM((pairs, blk, blk), BF16),
            pltpu.VMEM((pairs, blk, blk), BF16),
            pltpu.VMEM((pairs, blk, blk), F32),
            pltpu.SemaphoreType.DMA((8, 2)),
            pltpu.SemaphoreType.DMA((8, 2)),
        ],
        compiler_params=pltpu.CompilerParams(
            collective_id=0, has_side_effects=True, vmem_limit_bytes=40 * 1024 * 1024
        ),
    )(
        pair_blocks,
        slab_send,
        tile_send,
        ids,
        position.reshape(3, nb, blk),
        velocity.reshape(3, nb, blk),
        live_mass,
        density.reshape(nb, blk),
        deviator.reshape(6, nb, blk),
        plastic.reshape(nb, blk),
        energy.reshape(nb, blk),
    )
    return motion.reshape(4, nb * blk), material.reshape(8, nb * blk)


def solution(mesh):
    placed = (
        P(None, ("slab", "tile")),
        P(None, ("slab", "tile")),
        P(("slab", "tile")),
        P(("slab", "tile")),
        P(None, ("slab", "tile")),
        P(("slab", "tile")),
        P(("slab", "tile")),
        P(("slab", "tile")),
        P(None, ("slab", "tile")),
        P(("slab", "tile")),
        P(None, ("slab", "tile")),
        P(None, ("slab", "tile")),
    )
    return jax.shard_map(
        functools.partial(body, (mesh.shape["slab"], mesh.shape["tile"])),
        mesh=mesh,
        in_specs=placed,
        out_specs=(P(None, ("slab", "tile")), P(None, ("slab", "tile"))),
        check_vma=False,
    )
```

```python
import functools
import math

import jax
import jax.numpy as jnp
from jax import lax
from jax.experimental import pallas as pl
from jax.experimental.pallas import tpu as pltpu
from jax.sharding import PartitionSpec as P

MESH = pl.DeviceIdType.MESH
F32 = jnp.float32
BF16 = jnp.bfloat16
SWEEPS = 3
UNROLL = 32
ROWS = 8
R1 = 5 * ROWS
R2 = 9 * ROWS


SMOOTHING = 1.0
KERNEL_SCALE = -105.0 / (16.0 * math.pi)
TIME_STEP = 0.05
SHEAR_MODULUS = 1.0
BULK_MODULUS = 2.0
DENSITY_REF = 1.0
YIELD_BASE = 0.3
HARDEN_COEF = 2.0
HARDEN_EXPONENT = 0.31
RATE_COEF = 0.025
RATE_REF = 0.02
THERMAL_EXPONENT = 1.09
ENERGY_REF = 1.0
VISCOUS_ALPHA = 1.0
VISCOUS_BETA = 2.0
SOFTENING = 0.01
STRESS_FLOOR = 0.1


def power(base, exponent):
    return jnp.exp(exponent * jnp.log(base))


def sym_matrix(components):
    return [
        [components[0], components[3], components[5]],
        [components[3], components[1], components[4]],
        [components[5], components[4], components[2]],
    ]


def update_material(velocity_grad, deviator, plastic, energy, density):
    gradient_rows = [[velocity_grad[3 * a + b] for b in range(3)] for a in range(3)]
    strain = [
        [0.5 * (gradient_rows[a][b] + gradient_rows[b][a]) for b in range(3)] for a in range(3)
    ]
    rotation = [
        [0.5 * (gradient_rows[a][b] - gradient_rows[b][a]) for b in range(3)] for a in range(3)
    ]
    trace_rate = strain[0][0] + strain[1][1] + strain[2][2]
    new_density = density * jnp.exp(-TIME_STEP * trace_rate)
    mean_normal = (deviator[0] + deviator[1] + deviator[2]) / 3.0
    previous = sym_matrix(
        [
            deviator[0] - mean_normal,
            deviator[1] - mean_normal,
            deviator[2] - mean_normal,
            deviator[3],
            deviator[4],
            deviator[5],
        ]
    )
    shear_rate = [
        [strain[a][b] - trace_rate / 3.0 if a == b else strain[a][b] for b in range(3)]
        for a in range(3)
    ]
    trial_stress = []
    for a in range(3):
        trial_row = []
        for b in range(3):
            rate_term = 2.0 * SHEAR_MODULUS * shear_rate[a][b]
            for k in range(3):
                rate_term = (
                    rate_term + rotation[a][k] * previous[k][b] - previous[a][k] * rotation[k][b]
                )
            trial_row.append(previous[a][b] + TIME_STEP * rate_term)
        trial_stress.append(trial_row)
    trial_parts = [
        trial_stress[0][0],
        trial_stress[1][1],
        trial_stress[2][2],
        trial_stress[0][1],
        trial_stress[1][2],
        trial_stress[2][0],
    ]
    contract = (
        trial_parts[0] * trial_parts[0]
        + trial_parts[1] * trial_parts[1]
        + trial_parts[2] * trial_parts[2]
        + 2.0
        * (
            trial_parts[3] * trial_parts[3]
            + trial_parts[4] * trial_parts[4]
            + trial_parts[5] * trial_parts[5]
        )
    )
    equivalent = jnp.sqrt(1.5 * contract)
    rate_square = shear_rate[0][0] * shear_rate[0][0]
    for a in range(3):
        for b in range(3):
            if a + b > 0:
                rate_square = rate_square + shear_rate[a][b] * shear_rate[a][b]
    rate_equiv = jnp.sqrt(2.0 / 3.0 * rate_square)
    rate_factor = 1.0 + RATE_COEF * jnp.log(jnp.maximum(rate_equiv / RATE_REF, 1.0))
    homologous = energy / (energy + ENERGY_REF)
    scale_now = rate_factor * (1.0 - power(homologous, THERMAL_EXPONENT))
    tangent = (
        3.0 * SHEAR_MODULUS
        + HARDEN_COEF * HARDEN_EXPONENT * power(plastic, HARDEN_EXPONENT - 1.0) * scale_now
    )
    increment = jnp.zeros_like(plastic)
    for sweep_index in range(SWEEPS):
        flow_stress = (
            YIELD_BASE + HARDEN_COEF * power(plastic + increment, HARDEN_EXPONENT)
        ) * scale_now
        increment = jnp.maximum(
            increment + (equivalent - 3.0 * SHEAR_MODULUS * increment - flow_stress) / tangent, 0.0
        )
    shrink = 1.0 - 3.0 * SHEAR_MODULUS * increment / jnp.maximum(equivalent, STRESS_FLOOR)
    new_deviator = [component * shrink for component in trial_parts]
    pressure = BULK_MODULUS * (new_density / DENSITY_REF - 1.0)
    inverse_sq = 1.0 / (new_density * new_density)
    scaled = [
        (new_deviator[k] - pressure) * inverse_sq if k < 3 else new_deviator[k] * inverse_sq
        for k in range(6)
    ]
    sound_speed = jnp.sqrt((BULK_MODULUS + 4.0 / 3.0 * SHEAR_MODULUS) / new_density)
    return (new_deviator, plastic + increment, new_density, scaled, sound_speed)


def split_two(value):
    high = value.astype(BF16)
    return (high, (value - high.astype(F32)).astype(BF16))


def split_three(value):
    one = value.astype(BF16).astype(F32)
    rest = value - one
    two = rest.astype(BF16).astype(F32)
    return (one, two, rest - two)


def dot(left, right, contract=(1, 0)):
    return lax.dot_general(
        left, right, (((contract[0],), (contract[1],)), ((), ())), preferred_element_type=F32
    )


def reciprocal(value):
    guess = pl.reciprocal(value, approx=True)
    return guess * (2.0 - value * guess)


def sum_groups(row, first_value, second_value):
    f, s = split_three(first_value), split_three(second_value)
    left = jnp.where(row < 6, 1.0, 0.0)
    right = left
    for k in range(3):
        left = jnp.where(row == k, f[k], left)
        right = jnp.where(row == 3 + k, s[k], right)
    return left, right


def xyz_dot(row, left, right):
    return jnp.sum(jnp.where(row < 3, left * right, 0.0), axis=0, keepdims=True)


def swap(row, tile):
    return jnp.where(row < 3, pltpu.roll(tile, 5, 0), pltpu.roll(tile, 3, 0))


def centred(row, tile, centre):
    moved = jnp.where(row < 6, tile - centre, 1.0)
    along = xyz_dot(row, moved, swap(row, moved))
    return jnp.where(row == 7, along, moved), along


def geometry(row, first, second, first_along, second_along):
    a1, a2, a3 = split_three(first)
    b1, b2, b3 = split_three(second)
    order = (b1, b2, b1, b2, b3, b1)
    near = jnp.where(row < 3, -2.0, 0.0)
    cross = jnp.where(row < 6, -1.0, 0.0)
    swapped = [swap(row, b) * cross for b in (b1, b2, b3)]
    swapped = (swapped[0], swapped[1], swapped[0], swapped[1], swapped[2], swapped[0])
    norm_left, norm_right = sum_groups(
        row, xyz_dot(row, first, first), xyz_dot(row, second, second)
    )
    along_left, along_right = sum_groups(row, first_along, second_along)
    zero = jnp.zeros_like(first)
    left = jnp.concatenate([a1, a1, a2, a2, a1, a3, norm_left, along_left], 0).astype(BF16)
    right_one = jnp.concatenate([b * near for b in order] + [norm_right, zero], 0)
    right_two = jnp.concatenate(list(swapped) + [zero, along_right], 0)
    right = jnp.concatenate([right_one, right_two], 1).astype(BF16)
    both = dot(left, right, (0, 0))
    width = first.shape[1]
    return both[:, :width], both[:, width:]


def weigh(columns, high, low, side):
    count = columns.shape[0]
    top, rest = split_two(columns)
    left = jnp.concatenate(
        [jnp.concatenate([top, top], 1), jnp.concatenate([rest, jnp.zeros_like(rest)], 1)], 0
    )
    both = dot(left, jnp.concatenate([high, low], side[1]), side)
    return both[:count] + both[count:]


def gradient_columns(tile, moved):
    volume = tile[7:8]
    base = moved * volume
    return jnp.concatenate([base] + [base * moved[3 + a : 4 + a] for a in range(3)], 0)


def force_columns(row, tile, moved, stress):
    mass = tile[6:7]
    base = moved * mass
    cols = sym_matrix([stress[1 + k : 2 + k] for k in range(6)])
    turned = jnp.zeros_like(moved)
    first_row = jnp.logical_or(row == 0, row == 3)
    second_row = jnp.logical_or(row == 1, row == 4)
    for b in range(3):
        column = jnp.where(first_row, cols[0][b], jnp.where(second_row, cols[1][b], cols[2][b]))
        turned = turned + column * jnp.where(row < 3, moved[b : b + 1], moved[3 + b : 4 + b])
    inner = jnp.zeros_like(mass)
    for a in range(3):
        inner = inner + moved[a : a + 1] * turned[3 + a : 4 + a]
    turned = jnp.where(row < 6, turned, inner)
    return jnp.concatenate(
        [base]
        + [base * moved[3 + a : 4 + a] for a in range(3)]
        + [stress * mass, turned * mass],
        0,
    )


def hot(ids, rows):
    where = lax.broadcasted_iota(jnp.int32, (rows, ids.shape[1]), 0)
    return jnp.where(where == ids, 1.0, 0.0).astype(BF16)


def place(one_hot, value):
    high, low = split_two(value)
    return dot(one_hot, high) + dot(one_hot, low)


class Exchange:
    def __init__(self, axis, size, stage, sends, lands, send_sem, recv_sem):
        self.me = lax.axis_index(axis)
        self.size = size
        self.lands = lands
        self.copies = [
            pltpu.make_async_remote_copy(
                src_ref=sends[d],
                dst_ref=lands[d],
                send_sem=send_sem.at[stage, d],
                recv_sem=recv_sem.at[stage, d],
                device_id={axis: self.me + (1, -1)[d]},
                device_id_type=MESH,
            )
            for d in range(2)
        ]

    def start(self):
        low, high = self.me > 0, self.me < self.size - 1
        pl.when(high)(self.copies[0].start)
        pl.when(low)(self.copies[1].start)

        @pl.when(jnp.logical_not(low))
        def _():
            self.lands[0][...] = jnp.zeros(self.lands[0].shape, F32)

        @pl.when(jnp.logical_not(high))
        def _():
            self.lands[1][...] = jnp.zeros(self.lands[1].shape, F32)

    def wait(self):
        low, high = self.me > 0, self.me < self.size - 1
        pl.when(low)(self.copies[0].wait_recv)
        pl.when(high)(self.copies[1].wait_recv)

    def finish(self):
        low, high = self.me > 0, self.me < self.size - 1
        pl.when(high)(self.copies[0].wait_send)
        pl.when(low)(self.copies[1].wait_send)


def step_kernel(
    sizes,
    pairs_ref,
    slab_ref,
    tile_ref,
    ids_ref,
    position,
    velocity,
    live_mass,
    density,
    deviator,
    plastic,
    energy,
    motion,
    material,
    own_rows,
    table,
    stress_table,
    outgoing,
    arrived,
    slots,
    sums,
    sums_arrived,
    pulls,
    pulls_arrived,
    near_high,
    near_low,
    closing_ref,
    send_sem,
    recv_sem,
):
    n_slab, n_tile, nb, gs, pairs = sizes
    blk = live_mass.shape[1]
    ext = nb + 2 * gs
    full = ext + 2 * gs
    axes = (("slab", n_slab), ("tile", n_tile))

    barrier = pltpu.get_barrier_semaphore()
    expected = 0
    for axis, size in axes:
        me = lax.axis_index(axis)
        for shift, there in ((1, me < size - 1), (-1, me > 0)):

            @pl.when(there)
            def _(axis=axis, me=me, shift=shift):
                pl.semaphore_signal(
                    barrier, inc=1, device_id={axis: me + shift}, device_id_type=MESH
                )

            expected = expected + there.astype(jnp.int32)

    def put(field, value):
        own_rows[pl.ds(field, nb, stride=ROWS), :] = value

    def put_own(ref):
        ref[:nb] = own_rows[...].reshape(nb, ROWS, blk)

    for k in range(3):
        put(k, position[k])
        put(3 + k, velocity[k])
    put(6, live_mass[...])
    put(7, live_mass[...] / density[...])

    def spread(ref, stage, before=None):
        for step, (axis, size) in enumerate(axes):
            ids = (slab_ref, tile_ref)[step]
            at = stage + step
            mine = 2 * (stage // 4) + step
            for d in range(2):
                for k in range(gs):
                    outgoing[mine, d, k] = ref[ids[1 - d, k]]
            if before is not None and step == 0:
                before()
            swapping = Exchange(
                axis,
                size,
                at,
                [outgoing.at[mine, d] for d in range(2)],
                [arrived.at[mine, d] for d in range(2)],
                send_sem,
                recv_sem,
            )
            swapping.start()
            swapping.wait()
            base = (nb, ext)[step]
            for d in range(2):
                ref[base + d * gs : base + (d + 1) * gs] = arrived[mine, d]
            swapping.finish()

    put_own(table)
    spread(table, 0, before=lambda: pl.semaphore_wait(barrier, expected))

    row = lax.broadcasted_iota(jnp.int32, (ROWS, blk), 0)

    def tiles(ref, p):
        return ref[pairs_ref[0, p]], ref[pairs_ref[1, p]]

    def moved_tiles(p):
        first, second = tiles(table, p)
        centre = jnp.mean(first, axis=1, keepdims=True)
        one, one_along = centred(row, first, centre)
        two, two_along = centred(row, second, centre)
        return first, second, one, two, one_along, two_along

    def keep(slot, width, value):
        slots[pl.ds(pl.multiple_of(slot * width, ROWS), width), :] = value

    def gradient_pair(p):
        first, second, one, two, one_along, two_along = moved_tiles(p)
        radius_sq, approach = geometry(row, one, two, one_along, two_along)
        radius_sq = jnp.maximum(radius_sq, 1e-30)
        spread_now = jnp.maximum(1.0 - 0.5 * (radius_sq * lax.rsqrt(radius_sq)), 0.0)
        high, low = split_two(spread_now * spread_now * spread_now)
        closing = jnp.minimum(approach, 0.0) * reciprocal(radius_sq + SOFTENING)
        to_first = weigh(gradient_columns(second, two), high, low, (1, 1))
        to_second = weigh(gradient_columns(first, one), high, low, (1, 0))

        def store():
            near_high[p] = high
            near_low[p] = low
            closing_ref[p] = closing
            keep(p, R1, jnp.concatenate([to_first, one], 0))
            keep(pairs + p, R1, jnp.concatenate([to_second, two], 0))

        return store

    def force_pair(p):
        first, second, one, two, one_along, two_along = moved_tiles(p)
        first_stress, second_stress = tiles(stress_table, p)
        sound_left, sound_right = sum_groups(row, first_stress[7:8], second_stress[7:8])
        rho_left, rho_right = sum_groups(row, first_stress[0:1], second_stress[0:1])
        zero = jnp.zeros_like(row, F32)
        right_one = jnp.concatenate([sound_right, zero], 0)
        right_two = jnp.concatenate([zero, rho_right], 0)
        totals = dot(
            jnp.concatenate([sound_left, rho_left], 0).astype(BF16),
            jnp.concatenate([right_one, right_two], 1).astype(BF16),
            (0, 0),
        )
        sound, rho = totals[:, :blk], totals[:, blk:]
        high, low = near_high[p], near_low[p]
        near = high.astype(F32) + low.astype(F32)
        closing = closing_ref[p]
        viscous = near * closing * (4.0 * closing - sound) * reciprocal(rho)
        drag_high, drag_low = split_two(viscous)
        from_second = force_columns(row, second, two, second_stress)
        from_first = force_columns(row, first, one, first_stress)
        to_first = [
            weigh(from_second, high, low, (1, 1)),
            weigh(from_second[:ROWS], drag_high, drag_low, (1, 1)),
        ]
        to_second = [
            weigh(from_first, high, low, (1, 0)),
            weigh(from_first[:ROWS], drag_high, drag_low, (1, 0)),
        ]

        def store():
            keep(p, R2, jnp.concatenate(to_first + [one, first_stress], 0))
            keep(pairs + p, R2, jnp.concatenate(to_second + [two, second_stress], 0))

        return store

    def all_pairs(one_pair):
        def some(step, carry):
            stores = [one_pair(step * UNROLL + k) for k in range(UNROLL)]
            for store in stores:
                store()
            return carry

        lax.fori_loop(0, pairs // UNROLL, some, 0)
        for p in range(pairs // UNROLL * UNROLL, pairs):
            one_pair(p)()

    pair_hot = hot(ids_ref[0:1, : 2 * pairs], full)
    tile_hot = hot(ids_ref[1:2, : 2 * gs], ext)
    slab_hot = hot(ids_ref[2:3, : 2 * gs], nb)

    def give_back(ref, landing, stage):
        width = ref.shape[0]
        for step, (axis, size) in ((1, axes[1]), (0, axes[0])):
            base = (nb, ext)[step]
            one_hot = (slab_hot, tile_hot)[step]
            at = stage + 1 - step
            swapping = Exchange(
                axis,
                size,
                at,
                [ref.at[:, pl.ds(base + gs, gs), :], ref.at[:, pl.ds(base, gs), :]],
                [landing.at[step, d] for d in range(2)],
                send_sem,
                recv_sem,
            )
            swapping.start()
            swapping.wait()
            for c in range(width):
                come = jnp.concatenate([landing[step, 0, c], landing[step, 1, c]], 0)
                ref[c, :base, :] = ref[c, :base, :] + place(one_hot, come)
            swapping.finish()

    all_pairs(gradient_pair)

    def slot_rows(r, width):
        return slots[pl.ds(r, 2 * pairs, stride=width), :]

    for a in range(3):
        speed = slot_rows(4 * ROWS + 3 + a, R1)
        plain = slot_rows((a + 1) * ROWS + 6, R1) - speed * slot_rows(6, R1)
        for b in range(3):
            bent = slot_rows((a + 1) * ROWS + b, R1) - speed * slot_rows(b, R1)
            sums[3 * a + b] = place(pair_hot, slot_rows(4 * ROWS + b, R1) * plain - bent)
    give_back(sums, sums_arrived, 2)

    velocity_grad = [sums[c, :nb, :] * KERNEL_SCALE for c in range(9)]
    new_deviator, new_plastic, new_density, scaled, sound_speed = update_material(
        velocity_grad, [deviator[k] for k in range(6)], plastic[...], energy[...], density[...]
    )
    for k in range(6):
        material[k] = new_deviator[k]
        put(1 + k, scaled[k])
    material[6] = new_plastic
    material[7] = new_density
    put(0, new_density)
    put(7, sound_speed)
    put_own(stress_table)
    spread(stress_table, 4)

    all_pairs(force_pair)

    def get(r):
        return slot_rows(r, R2)

    place_of = [get(7 * ROWS + k) for k in range(3)]
    own = sym_matrix([get(8 * ROWS + 1 + k) for k in range(6)])
    other = sym_matrix([get(4 * ROWS + 1 + k) for k in range(6)])
    weight = get(6)
    drag = get(6 * ROWS + 6)
    heat = jnp.zeros_like(weight)
    bent = [place_of[b] * weight - get(b) for b in range(3)]
    for a in range(3):
        speed = get(7 * ROWS + 3 + a)
        carried = get(3 + a)
        pull = get(6 * ROWS + a) - place_of[a] * drag - get(5 * ROWS + a)
        inner = place_of[a] * (get(5 * ROWS + 3 + a) - get(6 * ROWS + 3 + a))
        for b in range(3):
            pull = pull + own[a][b] * bent[b] + other[a][b] * place_of[b]
            inner = inner + own[a][b] * (place_of[b] * carried - get((a + 1) * ROWS + b))
        heat = heat + speed * pull - inner
        pulls[a] = place(pair_hot, pull)
    heat = heat + get(5 * ROWS + 6) - get(6 * ROWS + 7)
    pulls[3] = place(pair_hot, heat)
    give_back(pulls, pulls_arrived, 6)
    for k in range(3):
        motion[k] = pulls[k, :nb, :] * KERNEL_SCALE
    motion[3] = pulls[3, :nb, :] * (-0.5 * KERNEL_SCALE)


def body(
    sizes,
    position,
    velocity,
    particle_mass,
    density,
    deviator,
    plastic,
    energy,
    block_fill,
    pair_blocks,
    pair_count,
    slab_send,
    tile_send,
):
    n_slab, n_tile = sizes
    nb = block_fill.shape[0]
    blk = position.shape[1] // nb
    gs = slab_send.shape[1]
    pairs = pair_blocks.shape[1]
    full = nb + 4 * gs
    alive = lax.broadcasted_iota(jnp.int32, (nb, blk), 1) < block_fill[:, None]
    live_mass = jnp.where(alive, particle_mass.reshape(nb, blk), 0.0)
    first, second = pair_blocks[0], pair_blocks[1]
    live = jnp.arange(pairs, dtype=jnp.int32) < pair_count[0]
    lane = max(2 * pairs, 2 * gs)

    def line(values):
        return jnp.pad(values, (0, lane - values.shape[0]), constant_values=-1)

    ids = jnp.stack(
        [
            line(
                jnp.concatenate(
                    [
                        jnp.where(live, first, -1),
                        jnp.where(live & (first != second), second, -1),
                    ]
                )
            ),
            line(tile_send.reshape(-1)),
            line(slab_send.reshape(-1)),
        ]
    )
    smem = pl.BlockSpec(memory_space=pltpu.SMEM)
    vmem = pl.BlockSpec(memory_space=pltpu.VMEM)
    motion, material = pl.pallas_call(
        functools.partial(step_kernel, (n_slab, n_tile, nb, gs, pairs)),
        out_shape=(
            jax.ShapeDtypeStruct((4, nb, blk), F32),
            jax.ShapeDtypeStruct((8, nb, blk), F32),
        ),
        in_specs=[smem] * 3 + [vmem] * 8,
        out_specs=(vmem, vmem),
        scratch_shapes=[
            pltpu.VMEM((nb * ROWS, blk), F32),
            pltpu.VMEM((full, ROWS, blk), F32),
            pltpu.VMEM((full, ROWS, blk), F32),
            pltpu.VMEM((4, 2, gs, ROWS, blk), F32),
            pltpu.VMEM((4, 2, gs, ROWS, blk), F32),
            pltpu.VMEM((2 * pairs * R2, blk), F32),
            pltpu.VMEM((9, full, blk), F32),
            pltpu.VMEM((2, 2, 9, gs, blk), F32),
            pltpu.VMEM((4, full, blk), F32),
            pltpu.VMEM((2, 2, 4, gs, blk), F32),
            pltpu.VMEM((pairs, blk, blk), BF16),
            pltpu.VMEM((pairs, blk, blk), BF16),
            pltpu.VMEM((pairs, blk, blk), F32),
            pltpu.SemaphoreType.DMA((8, 2)),
            pltpu.SemaphoreType.DMA((8, 2)),
        ],
        compiler_params=pltpu.CompilerParams(
            collective_id=0, has_side_effects=True, vmem_limit_bytes=40 * 1024 * 1024
        ),
    )(
        pair_blocks,
        slab_send,
        tile_send,
        ids,
        position.reshape(3, nb, blk),
        velocity.reshape(3, nb, blk),
        live_mass,
        density.reshape(nb, blk),
        deviator.reshape(6, nb, blk),
        plastic.reshape(nb, blk),
        energy.reshape(nb, blk),
    )
    return motion.reshape(4, nb * blk), material.reshape(8, nb * blk)


def solution(mesh):
    placed = (
        P(None, ("slab", "tile")),
        P(None, ("slab", "tile")),
        P(("slab", "tile")),
        P(("slab", "tile")),
        P(None, ("slab", "tile")),
        P(("slab", "tile")),
        P(("slab", "tile")),
        P(("slab", "tile")),
        P(None, ("slab", "tile")),
        P(("slab", "tile")),
        P(None, ("slab", "tile")),
        P(None, ("slab", "tile")),
    )
    return jax.shard_map(
        functools.partial(body, (mesh.shape["slab"], mesh.shape["tile"])),
        mesh=mesh,
        in_specs=placed,
        out_specs=(P(None, ("slab", "tile")), P(None, ("slab", "tile"))),
        check_vma=False,
    )
```

```python
import functools
import math

import jax
import jax.numpy as jnp
from jax import lax
from jax.experimental import pallas as pl
from jax.experimental.pallas import tpu as pltpu
from jax.sharding import PartitionSpec as P

MESH = pl.DeviceIdType.MESH
F32 = jnp.float32
BF16 = jnp.bfloat16
SWEEPS = 3
UNROLL = 32
ROWS = 8
R1 = 5 * ROWS
R2 = 9 * ROWS


SMOOTHING = 1.0
KERNEL_SCALE = -105.0 / (16.0 * math.pi)
TIME_STEP = 0.05
SHEAR_MODULUS = 1.0
BULK_MODULUS = 2.0
DENSITY_REF = 1.0
YIELD_BASE = 0.3
HARDEN_COEF = 2.0
HARDEN_EXPONENT = 0.31
RATE_COEF = 0.025
RATE_REF = 0.02
THERMAL_EXPONENT = 1.09
ENERGY_REF = 1.0
VISCOUS_ALPHA = 1.0
VISCOUS_BETA = 2.0
SOFTENING = 0.01
STRESS_FLOOR = 0.1


def power(base, exponent):
    return jnp.exp(exponent * jnp.log(base))


def sym_matrix(components):
    return [
        [components[0], components[3], components[5]],
        [components[3], components[1], components[4]],
        [components[5], components[4], components[2]],
    ]


def update_material(velocity_grad, deviator, plastic, energy, density):
    gradient_rows = [[velocity_grad[3 * a + b] for b in range(3)] for a in range(3)]
    strain = [
        [0.5 * (gradient_rows[a][b] + gradient_rows[b][a]) for b in range(3)] for a in range(3)
    ]
    rotation = [
        [0.5 * (gradient_rows[a][b] - gradient_rows[b][a]) for b in range(3)] for a in range(3)
    ]
    trace_rate = strain[0][0] + strain[1][1] + strain[2][2]
    new_density = density * jnp.exp(-TIME_STEP * trace_rate)
    mean_normal = (deviator[0] + deviator[1] + deviator[2]) / 3.0
    previous = sym_matrix(
        [
            deviator[0] - mean_normal,
            deviator[1] - mean_normal,
            deviator[2] - mean_normal,
            deviator[3],
            deviator[4],
            deviator[5],
        ]
    )
    shear_rate = [
        [strain[a][b] - trace_rate / 3.0 if a == b else strain[a][b] for b in range(3)]
        for a in range(3)
    ]
    trial_stress = []
    for a in range(3):
        trial_row = []
        for b in range(3):
            rate_term = 2.0 * SHEAR_MODULUS * shear_rate[a][b]
            for k in range(3):
                rate_term = (
                    rate_term + rotation[a][k] * previous[k][b] - previous[a][k] * rotation[k][b]
                )
            trial_row.append(previous[a][b] + TIME_STEP * rate_term)
        trial_stress.append(trial_row)
    trial_parts = [
        trial_stress[0][0],
        trial_stress[1][1],
        trial_stress[2][2],
        trial_stress[0][1],
        trial_stress[1][2],
        trial_stress[2][0],
    ]
    contract = (
        trial_parts[0] * trial_parts[0]
        + trial_parts[1] * trial_parts[1]
        + trial_parts[2] * trial_parts[2]
        + 2.0
        * (
            trial_parts[3] * trial_parts[3]
            + trial_parts[4] * trial_parts[4]
            + trial_parts[5] * trial_parts[5]
        )
    )
    equivalent = jnp.sqrt(1.5 * contract)
    rate_square = shear_rate[0][0] * shear_rate[0][0]
    for a in range(3):
        for b in range(3):
            if a + b > 0:
                rate_square = rate_square + shear_rate[a][b] * shear_rate[a][b]
    rate_equiv = jnp.sqrt(2.0 / 3.0 * rate_square)
    rate_factor = 1.0 + RATE_COEF * jnp.log(jnp.maximum(rate_equiv / RATE_REF, 1.0))
    homologous = energy / (energy + ENERGY_REF)
    scale_now = rate_factor * (1.0 - power(homologous, THERMAL_EXPONENT))
    tangent = (
        3.0 * SHEAR_MODULUS
        + HARDEN_COEF * HARDEN_EXPONENT * power(plastic, HARDEN_EXPONENT - 1.0) * scale_now
    )
    increment = jnp.zeros_like(plastic)
    for sweep_index in range(SWEEPS):
        flow_stress = (
            YIELD_BASE + HARDEN_COEF * power(plastic + increment, HARDEN_EXPONENT)
        ) * scale_now
        increment = jnp.maximum(
            increment + (equivalent - 3.0 * SHEAR_MODULUS * increment - flow_stress) / tangent, 0.0
        )
    shrink = 1.0 - 3.0 * SHEAR_MODULUS * increment / jnp.maximum(equivalent, STRESS_FLOOR)
    new_deviator = [component * shrink for component in trial_parts]
    pressure = BULK_MODULUS * (new_density / DENSITY_REF - 1.0)
    inverse_sq = 1.0 / (new_density * new_density)
    scaled = [
        (new_deviator[k] - pressure) * inverse_sq if k < 3 else new_deviator[k] * inverse_sq
        for k in range(6)
    ]
    sound_speed = jnp.sqrt((BULK_MODULUS + 4.0 / 3.0 * SHEAR_MODULUS) / new_density)
    return (new_deviator, plastic + increment, new_density, scaled, sound_speed)


def split_two(value):
    high = value.astype(BF16)
    return (high, (value - high.astype(F32)).astype(BF16))


def split_three(value):
    one = value.astype(BF16).astype(F32)
    rest = value - one
    two = rest.astype(BF16).astype(F32)
    return (one, two, rest - two)


def dot(left, right, contract=(1, 0)):
    return lax.dot_general(
        left, right, (((contract[0],), (contract[1],)), ((), ())), preferred_element_type=F32
    )


def reciprocal(value):
    guess = pl.reciprocal(value, approx=True)
    return guess * (2.0 - value * guess)


def sum_groups(row, first_value, second_value):
    f, s = split_three(first_value), split_three(second_value)
    left = jnp.where(row < 6, 1.0, 0.0)
    right = left
    for k in range(3):
        left = jnp.where(row == k, f[k], left)
        right = jnp.where(row == 3 + k, s[k], right)
    return left, right


def xyz_dot(row, left, right):
    return jnp.sum(jnp.where(row < 3, left * right, 0.0), axis=0, keepdims=True)


def swap(row, tile):
    return jnp.where(row < 3, pltpu.roll(tile, 5, 0), pltpu.roll(tile, 3, 0))


def centred(row, tile, centre):
    moved = jnp.where(row < 6, tile - centre, 1.0)
    along = xyz_dot(row, moved, swap(row, moved))
    return jnp.where(row == 7, along, moved), along


def geometry(row, first, second, first_along, second_along):
    a1, a2, a3 = split_three(first)
    b1, b2, b3 = split_three(second)
    order = (b1, b2, b1, b2, b3, b1)
    near = jnp.where(row < 3, -2.0, 0.0)
    cross = jnp.where(row < 6, -1.0, 0.0)
    swapped = [swap(row, b) * cross for b in (b1, b2, b3)]
    swapped = (swapped[0], swapped[1], swapped[0], swapped[1], swapped[2], swapped[0])
    norm_left, norm_right = sum_groups(
        row, xyz_dot(row, first, first), xyz_dot(row, second, second)
    )
    along_left, along_right = sum_groups(row, first_along, second_along)
    zero = jnp.zeros_like(first)
    left = jnp.concatenate([a1, a1, a2, a2, a1, a3, norm_left, along_left], 0).astype(BF16)
    right_one = jnp.concatenate([b * near for b in order] + [norm_right, zero], 0)
    right_two = jnp.concatenate(list(swapped) + [zero, along_right], 0)
    right = jnp.concatenate([right_one, right_two], 1).astype(BF16)
    both = dot(left, right, (0, 0))
    width = first.shape[1]
    return both[:, :width], both[:, width:]


def weigh(columns, high, low, side):
    count = columns.shape[0]
    top, rest = split_two(columns)
    left = jnp.concatenate(
        [jnp.concatenate([top, top], 1), jnp.concatenate([rest, jnp.zeros_like(rest)], 1)], 0
    )
    both = dot(left, jnp.concatenate([high, low], side[1]), side)
    return both[:count] + both[count:]


def gradient_columns(tile, moved):
    volume = tile[7:8]
    base = moved * volume
    return jnp.concatenate([base] + [base * moved[3 + a : 4 + a] for a in range(3)], 0)


def force_columns(row, tile, moved, stress):
    mass = tile[6:7]
    base = moved * mass
    cols = sym_matrix([stress[1 + k : 2 + k] for k in range(6)])
    turned = jnp.zeros_like(moved)
    first_row = jnp.logical_or(row == 0, row == 3)
    second_row = jnp.logical_or(row == 1, row == 4)
    for b in range(3):
        column = jnp.where(first_row, cols[0][b], jnp.where(second_row, cols[1][b], cols[2][b]))
        turned = turned + column * jnp.where(row < 3, moved[b : b + 1], moved[3 + b : 4 + b])
    inner = jnp.zeros_like(mass)
    for a in range(3):
        inner = inner + moved[a : a + 1] * turned[3 + a : 4 + a]
    turned = jnp.where(row < 6, turned, inner)
    return jnp.concatenate(
        [base]
        + [base * moved[3 + a : 4 + a] for a in range(3)]
        + [stress * mass, turned * mass],
        0,
    )


def hot(ids, rows):
    where = lax.broadcasted_iota(jnp.int32, (rows, ids.shape[1]), 0)
    return jnp.where(where == ids, 1.0, 0.0).astype(BF16)


def place(one_hot, value):
    high, low = split_two(value)
    return dot(one_hot, high) + dot(one_hot, low)


class Exchange:
    def __init__(self, axis, size, stage, sends, lands, send_sem, recv_sem):
        self.me = lax.axis_index(axis)
        self.size = size
        self.lands = lands
        self.copies = [
            pltpu.make_async_remote_copy(
                src_ref=sends[d],
                dst_ref=lands[d],
                send_sem=send_sem.at[stage, d],
                recv_sem=recv_sem.at[stage, d],
                device_id={axis: self.me + (1, -1)[d]},
                device_id_type=MESH,
            )
            for d in range(2)
        ]

    def start(self):
        low, high = self.me > 0, self.me < self.size - 1
        pl.when(high)(self.copies[0].start)
        pl.when(low)(self.copies[1].start)

        @pl.when(jnp.logical_not(low))
        def _():
            self.lands[0][...] = jnp.zeros(self.lands[0].shape, F32)

        @pl.when(jnp.logical_not(high))
        def _():
            self.lands[1][...] = jnp.zeros(self.lands[1].shape, F32)

    def wait(self):
        low, high = self.me > 0, self.me < self.size - 1
        pl.when(low)(self.copies[0].wait_recv)
        pl.when(high)(self.copies[1].wait_recv)

    def finish(self):
        low, high = self.me > 0, self.me < self.size - 1
        pl.when(high)(self.copies[0].wait_send)
        pl.when(low)(self.copies[1].wait_send)


def step_kernel(
    sizes,
    pairs_ref,
    slab_ref,
    tile_ref,
    ids_ref,
    position,
    velocity,
    live_mass,
    density,
    deviator,
    plastic,
    energy,
    motion,
    material,
    own_rows,
    table,
    stress_table,
    outgoing,
    arrived,
    slots,
    sums,
    sums_arrived,
    pulls,
    pulls_arrived,
    near_high,
    near_low,
    closing_ref,
    send_sem,
    recv_sem,
):
    n_slab, n_tile, nb, gs, pairs = sizes
    blk = live_mass.shape[1]
    ext = nb + 2 * gs
    full = ext + 2 * gs
    axes = (("slab", n_slab), ("tile", n_tile))

    barrier = pltpu.get_barrier_semaphore()
    expected = 0
    for axis, size in axes:
        me = lax.axis_index(axis)
        for shift, there in ((1, me < size - 1), (-1, me > 0)):

            @pl.when(there)
            def _(axis=axis, me=me, shift=shift):
                pl.semaphore_signal(
                    barrier, inc=1, device_id={axis: me + shift}, device_id_type=MESH
                )

            expected = expected + there.astype(jnp.int32)

    def put(field, value):
        own_rows[pl.ds(field, nb, stride=ROWS), :] = value

    def put_own(ref):
        ref[:nb] = own_rows[...].reshape(nb, ROWS, blk)

    for k in range(3):
        put(k, position[k])
        put(3 + k, velocity[k])
    put(6, live_mass[...])
    put(7, live_mass[...] / density[...])

    def spread(ref, stage, before=None):
        for step, (axis, size) in enumerate(axes):
            ids = (slab_ref, tile_ref)[step]
            at = stage + step
            mine = 2 * (stage // 4) + step
            for d in range(2):
                for k in range(gs):
                    outgoing[mine, d, k] = ref[ids[1 - d, k]]
            if before is not None and step == 0:
                before()
            swapping = Exchange(
                axis,
                size,
                at,
                [outgoing.at[mine, d] for d in range(2)],
                [arrived.at[mine, d] for d in range(2)],
                send_sem,
                recv_sem,
            )
            swapping.start()
            swapping.wait()
            base = (nb, ext)[step]
            for d in range(2):
                ref[base + d * gs : base + (d + 1) * gs] = arrived[mine, d]
            swapping.finish()

    put_own(table)
    spread(table, 0, before=lambda: pl.semaphore_wait(barrier, expected))

    row = lax.broadcasted_iota(jnp.int32, (ROWS, blk), 0)

    def tiles(ref, p):
        return ref[pairs_ref[0, p]], ref[pairs_ref[1, p]]

    def moved_tiles(p):
        first, second = tiles(table, p)
        centre = jnp.mean(first, axis=1, keepdims=True)
        one, one_along = centred(row, first, centre)
        two, two_along = centred(row, second, centre)
        return first, second, one, two, one_along, two_along

    def keep(slot, width, value):
        slots[pl.ds(pl.multiple_of(slot * width, ROWS), width), :] = value

    def gradient_pair(p):
        first, second, one, two, one_along, two_along = moved_tiles(p)
        radius_sq, approach = geometry(row, one, two, one_along, two_along)
        radius_sq = jnp.maximum(radius_sq, 1e-30)
        spread_now = jnp.maximum(1.0 - 0.5 * (radius_sq * lax.rsqrt(radius_sq)), 0.0)
        high, low = split_two(spread_now * spread_now * spread_now)
        closing = jnp.minimum(approach, 0.0) * reciprocal(radius_sq + SOFTENING)
        to_first = weigh(gradient_columns(second, two), high, low, (1, 1))
        to_second = weigh(gradient_columns(first, one), high, low, (1, 0))

        def store():
            near_high[p] = high
            near_low[p] = low
            closing_ref[p] = closing
            keep(p, R1, jnp.concatenate([to_first, one], 0))
            keep(pairs + p, R1, jnp.concatenate([to_second, two], 0))

        return store

    def force_pair(p):
        first, second, one, two, one_along, two_along = moved_tiles(p)
        first_stress, second_stress = tiles(stress_table, p)
        sound_left, sound_right = sum_groups(row, first_stress[7:8], second_stress[7:8])
        rho_left, rho_right = sum_groups(row, first_stress[0:1], second_stress[0:1])
        zero = jnp.zeros_like(row, F32)
        right_one = jnp.concatenate([sound_right, zero], 0)
        right_two = jnp.concatenate([zero, rho_right], 0)
        totals = dot(
            jnp.concatenate([sound_left, rho_left], 0).astype(BF16),
            jnp.concatenate([right_one, right_two], 1).astype(BF16),
            (0, 0),
        )
        sound, rho = totals[:, :blk], totals[:, blk:]
        high, low = near_high[p], near_low[p]
        near = high.astype(F32) + low.astype(F32)
        closing = closing_ref[p]
        viscous = near * closing * (4.0 * closing - sound) * reciprocal(rho)
        drag_high, drag_low = split_two(viscous)
        from_second = force_columns(row, second, two, second_stress)
        from_first = force_columns(row, first, one, first_stress)
        to_first = [
            weigh(from_second, high, low, (1, 1)),
            weigh(from_second[:ROWS], drag_high, drag_low, (1, 1)),
        ]
        to_second = [
            weigh(from_first, high, low, (1, 0)),
            weigh(from_first[:ROWS], drag_high, drag_low, (1, 0)),
        ]

        def store():
            keep(p, R2, jnp.concatenate(to_first + [one, first_stress], 0))
            keep(pairs + p, R2, jnp.concatenate(to_second + [two, second_stress], 0))

        return store

    def all_pairs(one_pair):
        def some(step, carry):
            stores = [one_pair(step * UNROLL + k) for k in range(UNROLL)]
            for store in stores:
                store()
            return carry

        lax.fori_loop(0, pairs // UNROLL, some, 0)
        for p in range(pairs // UNROLL * UNROLL, pairs):
            one_pair(p)()

    pair_hot = hot(ids_ref[0:1, : 2 * pairs], full)
    tile_hot = hot(ids_ref[1:2, : 2 * gs], ext)
    slab_hot = hot(ids_ref[2:3, : 2 * gs], nb)

    def add_arrived(ref, landing, step, one_hot, low, high):
        for c in range(ref.shape[0]):
            come = jnp.concatenate([landing[step, 0, c], landing[step, 1, c]], 0)
            ref[c, low:high, :] = ref[c, low:high, :] + place(one_hot[low:high], come)

    def give_back(ref, landing, stage, contributions):
        width = ref.shape[0]
        for c in range(width):
            ref[c, ext:, :] = place(pair_hot[ext:], contributions[c])
        for step, (axis, size) in ((1, axes[1]), (0, axes[0])):
            base = (nb, ext)[step]
            one_hot = (slab_hot, tile_hot)[step]
            at = stage + 1 - step
            swapping = Exchange(
                axis,
                size,
                at,
                [ref.at[:, pl.ds(base + gs, gs), :], ref.at[:, pl.ds(base, gs), :]],
                [landing.at[step, d] for d in range(2)],
                send_sem,
                recv_sem,
            )
            swapping.start()
            if step == 1:
                for c in range(width):
                    ref[c, :ext, :] = place(pair_hot[:ext], contributions[c])
            else:
                add_arrived(ref, landing, 1, tile_hot, 0, nb)
            swapping.wait()
            add_arrived(ref, landing, step, one_hot, nb * step, base)
            swapping.finish()

    all_pairs(gradient_pair)

    def slot_rows(r, width):
        return slots[pl.ds(r, 2 * pairs, stride=width), :]

    contributions = []
    for a in range(3):
        speed = slot_rows(4 * ROWS + 3 + a, R1)
        plain = slot_rows((a + 1) * ROWS + 6, R1) - speed * slot_rows(6, R1)
        for b in range(3):
            bent = slot_rows((a + 1) * ROWS + b, R1) - speed * slot_rows(b, R1)
            contributions.append(slot_rows(4 * ROWS + b, R1) * plain - bent)
    give_back(sums, sums_arrived, 2, contributions)

    velocity_grad = [sums[c, :nb, :] * KERNEL_SCALE for c in range(9)]
    new_deviator, new_plastic, new_density, scaled, sound_speed = update_material(
        velocity_grad, [deviator[k] for k in range(6)], plastic[...], energy[...], density[...]
    )
    for k in range(6):
        material[k] = new_deviator[k]
        put(1 + k, scaled[k])
    material[6] = new_plastic
    material[7] = new_density
    put(0, new_density)
    put(7, sound_speed)
    put_own(stress_table)
    spread(stress_table, 4)

    all_pairs(force_pair)

    def get(r):
        return slot_rows(r, R2)

    place_of = [get(7 * ROWS + k) for k in range(3)]
    own = sym_matrix([get(8 * ROWS + 1 + k) for k in range(6)])
    other = sym_matrix([get(4 * ROWS + 1 + k) for k in range(6)])
    weight = get(6)
    drag = get(6 * ROWS + 6)
    heat = jnp.zeros_like(weight)
    contributions = []
    bent = [place_of[b] * weight - get(b) for b in range(3)]
    for a in range(3):
        speed = get(7 * ROWS + 3 + a)
        carried = get(3 + a)
        pull = get(6 * ROWS + a) - place_of[a] * drag - get(5 * ROWS + a)
        inner = place_of[a] * (get(5 * ROWS + 3 + a) - get(6 * ROWS + 3 + a))
        for b in range(3):
            pull = pull + own[a][b] * bent[b] + other[a][b] * place_of[b]
            inner = inner + own[a][b] * (place_of[b] * carried - get((a + 1) * ROWS + b))
        heat = heat + speed * pull - inner
        contributions.append(pull)
    heat = heat + get(5 * ROWS + 6) - get(6 * ROWS + 7)
    contributions.append(heat)
    give_back(pulls, pulls_arrived, 6, contributions)
    for k in range(3):
        motion[k] = pulls[k, :nb, :] * KERNEL_SCALE
    motion[3] = pulls[3, :nb, :] * (-0.5 * KERNEL_SCALE)


def body(
    sizes,
    position,
    velocity,
    particle_mass,
    density,
    deviator,
    plastic,
    energy,
    block_fill,
    pair_blocks,
    pair_count,
    slab_send,
    tile_send,
):
    n_slab, n_tile = sizes
    nb = block_fill.shape[0]
    blk = position.shape[1] // nb
    gs = slab_send.shape[1]
    pairs = pair_blocks.shape[1]
    full = nb + 4 * gs
    alive = lax.broadcasted_iota(jnp.int32, (nb, blk), 1) < block_fill[:, None]
    live_mass = jnp.where(alive, particle_mass.reshape(nb, blk), 0.0)
    first, second = pair_blocks[0], pair_blocks[1]
    live = jnp.arange(pairs, dtype=jnp.int32) < pair_count[0]
    lane = max(2 * pairs, 2 * gs)

    def line(values):
        return jnp.pad(values, (0, lane - values.shape[0]), constant_values=-1)

    ids = jnp.stack(
        [
            line(
                jnp.concatenate(
                    [
                        jnp.where(live, first, -1),
                        jnp.where(live & (first != second), second, -1),
                    ]
                )
            ),
            line(tile_send.reshape(-1)),
            line(slab_send.reshape(-1)),
        ]
    )
    smem = pl.BlockSpec(memory_space=pltpu.SMEM)
    vmem = pl.BlockSpec(memory_space=pltpu.VMEM)
    motion, material = pl.pallas_call(
        functools.partial(step_kernel, (n_slab, n_tile, nb, gs, pairs)),
        out_shape=(
            jax.ShapeDtypeStruct((4, nb, blk), F32),
            jax.ShapeDtypeStruct((8, nb, blk), F32),
        ),
        in_specs=[smem] * 3 + [vmem] * 8,
        out_specs=(vmem, vmem),
        scratch_shapes=[
            pltpu.VMEM((nb * ROWS, blk), F32),
            pltpu.VMEM((full, ROWS, blk), F32),
            pltpu.VMEM((full, ROWS, blk), F32),
            pltpu.VMEM((4, 2, gs, ROWS, blk), F32),
            pltpu.VMEM((4, 2, gs, ROWS, blk), F32),
            pltpu.VMEM((2 * pairs * R2, blk), F32),
            pltpu.VMEM((9, full, blk), F32),
            pltpu.VMEM((2, 2, 9, gs, blk), F32),
            pltpu.VMEM((4, full, blk), F32),
            pltpu.VMEM((2, 2, 4, gs, blk), F32),
            pltpu.VMEM((pairs, blk, blk), BF16),
            pltpu.VMEM((pairs, blk, blk), BF16),
            pltpu.VMEM((pairs, blk, blk), F32),
            pltpu.SemaphoreType.DMA((8, 2)),
            pltpu.SemaphoreType.DMA((8, 2)),
        ],
        compiler_params=pltpu.CompilerParams(
            collective_id=0, has_side_effects=True, vmem_limit_bytes=40 * 1024 * 1024
        ),
    )(
        pair_blocks,
        slab_send,
        tile_send,
        ids,
        position.reshape(3, nb, blk),
        velocity.reshape(3, nb, blk),
        live_mass,
        density.reshape(nb, blk),
        deviator.reshape(6, nb, blk),
        plastic.reshape(nb, blk),
        energy.reshape(nb, blk),
    )
    return motion.reshape(4, nb * blk), material.reshape(8, nb * blk)


def solution(mesh):
    placed = (
        P(None, ("slab", "tile")),
        P(None, ("slab", "tile")),
        P(("slab", "tile")),
        P(("slab", "tile")),
        P(None, ("slab", "tile")),
        P(("slab", "tile")),
        P(("slab", "tile")),
        P(("slab", "tile")),
        P(None, ("slab", "tile")),
        P(("slab", "tile")),
        P(None, ("slab", "tile")),
        P(None, ("slab", "tile")),
    )
    return jax.shard_map(
        functools.partial(body, (mesh.shape["slab"], mesh.shape["tile"])),
        mesh=mesh,
        in_specs=placed,
        out_specs=(P(None, ("slab", "tile")), P(None, ("slab", "tile"))),
        check_vma=False,
    )
```

```python
import functools
import math

import jax
import jax.numpy as jnp
from jax import lax
from jax.experimental import pallas as pl
from jax.experimental.pallas import tpu as pltpu
from jax.sharding import PartitionSpec as P

MESH = pl.DeviceIdType.MESH
F32 = jnp.float32
BF16 = jnp.bfloat16
SWEEPS = 3
UNROLL = 32
ROWS = 8
R1 = 5 * ROWS
R2 = 9 * ROWS


SMOOTHING = 1.0
KERNEL_SCALE = -105.0 / (16.0 * math.pi)
TIME_STEP = 0.05
SHEAR_MODULUS = 1.0
BULK_MODULUS = 2.0
DENSITY_REF = 1.0
YIELD_BASE = 0.3
HARDEN_COEF = 2.0
HARDEN_EXPONENT = 0.31
RATE_COEF = 0.025
RATE_REF = 0.02
THERMAL_EXPONENT = 1.09
ENERGY_REF = 1.0
VISCOUS_ALPHA = 1.0
VISCOUS_BETA = 2.0
SOFTENING = 0.01
STRESS_FLOOR = 0.1


def power(base, exponent):
    return jnp.exp(exponent * jnp.log(base))


def sym_matrix(components):
    return [
        [components[0], components[3], components[5]],
        [components[3], components[1], components[4]],
        [components[5], components[4], components[2]],
    ]


def update_material(velocity_grad, deviator, plastic, energy, density):
    gradient_rows = [[velocity_grad[3 * a + b] for b in range(3)] for a in range(3)]
    strain = [
        [0.5 * (gradient_rows[a][b] + gradient_rows[b][a]) for b in range(3)] for a in range(3)
    ]
    rotation = [
        [0.5 * (gradient_rows[a][b] - gradient_rows[b][a]) for b in range(3)] for a in range(3)
    ]
    trace_rate = strain[0][0] + strain[1][1] + strain[2][2]
    new_density = density * jnp.exp(-TIME_STEP * trace_rate)
    mean_normal = (deviator[0] + deviator[1] + deviator[2]) / 3.0
    previous = sym_matrix(
        [
            deviator[0] - mean_normal,
            deviator[1] - mean_normal,
            deviator[2] - mean_normal,
            deviator[3],
            deviator[4],
            deviator[5],
        ]
    )
    shear_rate = [
        [strain[a][b] - trace_rate / 3.0 if a == b else strain[a][b] for b in range(3)]
        for a in range(3)
    ]
    trial_stress = []
    for a in range(3):
        trial_row = []
        for b in range(3):
            rate_term = 2.0 * SHEAR_MODULUS * shear_rate[a][b]
            for k in range(3):
                rate_term = (
                    rate_term + rotation[a][k] * previous[k][b] - previous[a][k] * rotation[k][b]
                )
            trial_row.append(previous[a][b] + TIME_STEP * rate_term)
        trial_stress.append(trial_row)
    trial_parts = [
        trial_stress[0][0],
        trial_stress[1][1],
        trial_stress[2][2],
        trial_stress[0][1],
        trial_stress[1][2],
        trial_stress[2][0],
    ]
    contract = (
        trial_parts[0] * trial_parts[0]
        + trial_parts[1] * trial_parts[1]
        + trial_parts[2] * trial_parts[2]
        + 2.0
        * (
            trial_parts[3] * trial_parts[3]
            + trial_parts[4] * trial_parts[4]
            + trial_parts[5] * trial_parts[5]
        )
    )
    equivalent = jnp.sqrt(1.5 * contract)
    rate_square = shear_rate[0][0] * shear_rate[0][0]
    for a in range(3):
        for b in range(3):
            if a + b > 0:
                rate_square = rate_square + shear_rate[a][b] * shear_rate[a][b]
    rate_equiv = jnp.sqrt(2.0 / 3.0 * rate_square)
    rate_factor = 1.0 + RATE_COEF * jnp.log(jnp.maximum(rate_equiv / RATE_REF, 1.0))
    homologous = energy / (energy + ENERGY_REF)
    scale_now = rate_factor * (1.0 - power(homologous, THERMAL_EXPONENT))
    tangent = (
        3.0 * SHEAR_MODULUS
        + HARDEN_COEF * HARDEN_EXPONENT * power(plastic, HARDEN_EXPONENT - 1.0) * scale_now
    )
    increment = jnp.zeros_like(plastic)
    for sweep_index in range(SWEEPS):
        flow_stress = (
            YIELD_BASE + HARDEN_COEF * power(plastic + increment, HARDEN_EXPONENT)
        ) * scale_now
        increment = jnp.maximum(
            increment + (equivalent - 3.0 * SHEAR_MODULUS * increment - flow_stress) / tangent, 0.0
        )
    shrink = 1.0 - 3.0 * SHEAR_MODULUS * increment / jnp.maximum(equivalent, STRESS_FLOOR)
    new_deviator = [component * shrink for component in trial_parts]
    pressure = BULK_MODULUS * (new_density / DENSITY_REF - 1.0)
    inverse_sq = 1.0 / (new_density * new_density)
    scaled = [
        (new_deviator[k] - pressure) * inverse_sq if k < 3 else new_deviator[k] * inverse_sq
        for k in range(6)
    ]
    sound_speed = jnp.sqrt((BULK_MODULUS + 4.0 / 3.0 * SHEAR_MODULUS) / new_density)
    return (new_deviator, plastic + increment, new_density, scaled, sound_speed)


def split_two(value):
    high = value.astype(BF16)
    return (high, (value - high.astype(F32)).astype(BF16))


def split_three(value):
    one = value.astype(BF16).astype(F32)
    rest = value - one
    two = rest.astype(BF16).astype(F32)
    return (one, two, rest - two)


def dot(left, right, contract=(1, 0)):
    return lax.dot_general(
        left, right, (((contract[0],), (contract[1],)), ((), ())), preferred_element_type=F32
    )


def reciprocal(value):
    guess = pl.reciprocal(value, approx=True)
    return guess * (2.0 - value * guess)


def sum_groups(row, first_value, second_value):
    f, s = split_three(first_value), split_three(second_value)
    left = jnp.where(row < 6, 1.0, 0.0)
    right = left
    for k in range(3):
        left = jnp.where(row == k, f[k], left)
        right = jnp.where(row == 3 + k, s[k], right)
    return left, right


def xyz_dot(row, left, right):
    return jnp.sum(jnp.where(row < 3, left * right, 0.0), axis=0, keepdims=True)


def swap(row, tile):
    return jnp.where(row < 3, pltpu.roll(tile, 5, 0), pltpu.roll(tile, 3, 0))


def centred(row, tile, centre):
    moved = jnp.where(row < 6, tile - centre, 1.0)
    along = xyz_dot(row, moved, swap(row, moved))
    return jnp.where(row == 7, along, moved), along


def geometry(row, first, second, first_along, second_along):
    a1, a2, a3 = split_three(first)
    b1, b2, b3 = split_three(second)
    order = (b1, b2, b1, b2, b3, b1)
    near = jnp.where(row < 3, -2.0, 0.0)
    cross = jnp.where(row < 6, -1.0, 0.0)
    swapped = [swap(row, b) * cross for b in (b1, b2, b3)]
    swapped = (swapped[0], swapped[1], swapped[0], swapped[1], swapped[2], swapped[0])
    norm_left, norm_right = sum_groups(
        row, xyz_dot(row, first, first), xyz_dot(row, second, second)
    )
    along_left, along_right = sum_groups(row, first_along, second_along)
    zero = jnp.zeros_like(first)
    left = jnp.concatenate([a1, a1, a2, a2, a1, a3, norm_left, along_left], 0).astype(BF16)
    right_one = jnp.concatenate([b * near for b in order] + [norm_right, zero], 0)
    right_two = jnp.concatenate(list(swapped) + [zero, along_right], 0)
    right = jnp.concatenate([right_one, right_two], 1).astype(BF16)
    both = dot(left, right, (0, 0))
    width = first.shape[1]
    return both[:, :width], both[:, width:]


def weigh(columns, high, low, side):
    count = columns.shape[0]
    top, rest = split_two(columns)
    left = jnp.concatenate(
        [jnp.concatenate([top, top], 1), jnp.concatenate([rest, jnp.zeros_like(rest)], 1)], 0
    )
    both = dot(left, jnp.concatenate([high, low], side[1]), side)
    return both[:count] + both[count:]


def gradient_columns(tile, moved):
    volume = tile[7:8]
    base = moved * volume
    return jnp.concatenate([base] + [base * moved[3 + a : 4 + a] for a in range(3)], 0)


def force_columns(row, tile, moved, stress):
    mass = tile[6:7]
    base = moved * mass
    cols = sym_matrix([stress[1 + k : 2 + k] for k in range(6)])
    turned = jnp.zeros_like(moved)
    first_row = jnp.logical_or(row == 0, row == 3)
    second_row = jnp.logical_or(row == 1, row == 4)
    for b in range(3):
        column = jnp.where(first_row, cols[0][b], jnp.where(second_row, cols[1][b], cols[2][b]))
        turned = turned + column * jnp.where(row < 3, moved[b : b + 1], moved[3 + b : 4 + b])
    inner = jnp.zeros_like(mass)
    for a in range(3):
        inner = inner + moved[a : a + 1] * turned[3 + a : 4 + a]
    turned = jnp.where(row < 6, turned, inner)
    return jnp.concatenate(
        [base]
        + [base * moved[3 + a : 4 + a] for a in range(3)]
        + [stress * mass, turned * mass],
        0,
    )


def hot(ids, rows):
    where = lax.broadcasted_iota(jnp.int32, (rows, ids.shape[1]), 0)
    return jnp.where(where == ids, 1.0, 0.0).astype(BF16)


def place(one_hot, value):
    high, low = split_two(value)
    return dot(one_hot, high) + dot(one_hot, low)


class Exchange:
    def __init__(self, axis, size, stage, sends, lands, send_sem, recv_sem):
        self.me = lax.axis_index(axis)
        self.size = size
        self.lands = lands
        self.copies = [
            pltpu.make_async_remote_copy(
                src_ref=sends[d],
                dst_ref=lands[d],
                send_sem=send_sem.at[stage, d],
                recv_sem=recv_sem.at[stage, d],
                device_id={axis: self.me + (1, -1)[d]},
                device_id_type=MESH,
            )
            for d in range(2)
        ]

    def start(self):
        low, high = self.me > 0, self.me < self.size - 1
        pl.when(high)(self.copies[0].start)
        pl.when(low)(self.copies[1].start)

        @pl.when(jnp.logical_not(low))
        def _():
            self.lands[0][...] = jnp.zeros(self.lands[0].shape, F32)

        @pl.when(jnp.logical_not(high))
        def _():
            self.lands[1][...] = jnp.zeros(self.lands[1].shape, F32)

    def wait(self):
        low, high = self.me > 0, self.me < self.size - 1
        pl.when(low)(self.copies[0].wait_recv)
        pl.when(high)(self.copies[1].wait_recv)

    def finish(self):
        low, high = self.me > 0, self.me < self.size - 1
        pl.when(high)(self.copies[0].wait_send)
        pl.when(low)(self.copies[1].wait_send)


def step_kernel(
    sizes,
    pairs_ref,
    slab_ref,
    tile_ref,
    ids_ref,
    position,
    velocity,
    live_mass,
    density,
    deviator,
    plastic,
    energy,
    motion,
    material,
    own_rows,
    table,
    stress_table,
    outgoing,
    arrived,
    slots,
    sums,
    sums_arrived,
    pulls,
    pulls_arrived,
    near_high,
    near_low,
    closing_ref,
    moved_ref,
    send_sem,
    recv_sem,
):
    n_slab, n_tile, nb, gs, pairs = sizes
    blk = live_mass.shape[1]
    ext = nb + 2 * gs
    full = ext + 2 * gs
    axes = (("slab", n_slab), ("tile", n_tile))

    barrier = pltpu.get_barrier_semaphore()
    expected = 0
    for axis, size in axes:
        me = lax.axis_index(axis)
        for shift, there in ((1, me < size - 1), (-1, me > 0)):

            @pl.when(there)
            def _(axis=axis, me=me, shift=shift):
                pl.semaphore_signal(
                    barrier, inc=1, device_id={axis: me + shift}, device_id_type=MESH
                )

            expected = expected + there.astype(jnp.int32)

    def put(field, value):
        own_rows[pl.ds(field, nb, stride=ROWS), :] = value

    def put_own(ref):
        ref[:nb] = own_rows[...].reshape(nb, ROWS, blk)

    for k in range(3):
        put(k, position[k])
        put(3 + k, velocity[k])
    put(6, live_mass[...])
    put(7, live_mass[...] / density[...])

    def spread(ref, stage, before=None):
        for step, (axis, size) in enumerate(axes):
            ids = (slab_ref, tile_ref)[step]
            at = stage + step
            mine = 2 * (stage // 4) + step
            for d in range(2):
                for k in range(gs):
                    outgoing[mine, d, k] = ref[ids[1 - d, k]]
            if before is not None and step == 0:
                before()
            swapping = Exchange(
                axis,
                size,
                at,
                [outgoing.at[mine, d] for d in range(2)],
                [arrived.at[mine, d] for d in range(2)],
                send_sem,
                recv_sem,
            )
            swapping.start()
            swapping.wait()
            base = (nb, ext)[step]
            for d in range(2):
                ref[base + d * gs : base + (d + 1) * gs] = arrived[mine, d]
            swapping.finish()

    put_own(table)
    spread(table, 0, before=lambda: pl.semaphore_wait(barrier, expected))

    row = lax.broadcasted_iota(jnp.int32, (ROWS, blk), 0)

    def tiles(ref, p):
        return ref[pairs_ref[0, p]], ref[pairs_ref[1, p]]

    def moved_tiles(p):
        first, second = tiles(table, p)
        centre = jnp.mean(first, axis=1, keepdims=True)
        one, one_along = centred(row, first, centre)
        two, two_along = centred(row, second, centre)
        return first, second, one, two, one_along, two_along

    def keep(slot, width, value):
        slots[pl.ds(pl.multiple_of(slot * width, ROWS), width), :] = value

    def gradient_pair(p):
        first, second, one, two, one_along, two_along = moved_tiles(p)
        radius_sq, approach = geometry(row, one, two, one_along, two_along)
        radius_sq = jnp.maximum(radius_sq, 1e-30)
        spread_now = jnp.maximum(1.0 - 0.5 * (radius_sq * lax.rsqrt(radius_sq)), 0.0)
        high, low = split_two(spread_now * spread_now * spread_now)
        closing = jnp.minimum(approach, 0.0) * reciprocal(radius_sq + SOFTENING)
        to_first = weigh(gradient_columns(second, two), high, low, (1, 1))
        to_second = weigh(gradient_columns(first, one), high, low, (1, 0))

        def store():
            near_high[p] = high
            near_low[p] = low
            closing_ref[p] = closing
            moved_ref[0, p] = one
            moved_ref[1, p] = two
            keep(p, R1, jnp.concatenate([to_first, one], 0))
            keep(pairs + p, R1, jnp.concatenate([to_second, two], 0))

        return store

    def force_pair(p):
        first, second = tiles(table, p)
        one, two = moved_ref[0, p], moved_ref[1, p]
        first_stress, second_stress = tiles(stress_table, p)
        sound_left, sound_right = sum_groups(row, first_stress[7:8], second_stress[7:8])
        rho_left, rho_right = sum_groups(row, first_stress[0:1], second_stress[0:1])
        zero = jnp.zeros_like(row, F32)
        right_one = jnp.concatenate([sound_right, zero], 0)
        right_two = jnp.concatenate([zero, rho_right], 0)
        totals = dot(
            jnp.concatenate([sound_left, rho_left], 0).astype(BF16),
            jnp.concatenate([right_one, right_two], 1).astype(BF16),
            (0, 0),
        )
        sound, rho = totals[:, :blk], totals[:, blk:]
        high, low = near_high[p], near_low[p]
        near = high.astype(F32) + low.astype(F32)
        closing = closing_ref[p]
        viscous = near * closing * (4.0 * closing - sound) * reciprocal(rho)
        drag_high, drag_low = split_two(viscous)
        from_second = force_columns(row, second, two, second_stress)
        from_first = force_columns(row, first, one, first_stress)
        to_first = [
            weigh(from_second, high, low, (1, 1)),
            weigh(from_second[:ROWS], drag_high, drag_low, (1, 1)),
        ]
        to_second = [
            weigh(from_first, high, low, (1, 0)),
            weigh(from_first[:ROWS], drag_high, drag_low, (1, 0)),
        ]

        def store():
            keep(p, R2, jnp.concatenate(to_first + [one, first_stress], 0))
            keep(pairs + p, R2, jnp.concatenate(to_second + [two, second_stress], 0))

        return store

    def all_pairs(one_pair):
        def some(step, carry):
            stores = [one_pair(step * UNROLL + k) for k in range(UNROLL)]
            for store in stores:
                store()
            return carry

        lax.fori_loop(0, pairs // UNROLL, some, 0)
        for p in range(pairs // UNROLL * UNROLL, pairs):
            one_pair(p)()

    pair_hot = hot(ids_ref[0:1, : 2 * pairs], full)
    tile_hot = hot(ids_ref[1:2, : 2 * gs], ext)
    slab_hot = hot(ids_ref[2:3, : 2 * gs], nb)

    def add_arrived(ref, landing, step, one_hot, low, high):
        for c in range(ref.shape[0]):
            come = jnp.concatenate([landing[step, 0, c], landing[step, 1, c]], 0)
            ref[c, low:high, :] = ref[c, low:high, :] + place(one_hot[low:high], come)

    def give_back(ref, landing, stage, contributions):
        width = ref.shape[0]
        for c in range(width):
            ref[c, ext:, :] = place(pair_hot[ext:], contributions[c])
        for step, (axis, size) in ((1, axes[1]), (0, axes[0])):
            base = (nb, ext)[step]
            one_hot = (slab_hot, tile_hot)[step]
            at = stage + 1 - step
            swapping = Exchange(
                axis,
                size,
                at,
                [ref.at[:, pl.ds(base + gs, gs), :], ref.at[:, pl.ds(base, gs), :]],
                [landing.at[step, d] for d in range(2)],
                send_sem,
                recv_sem,
            )
            swapping.start()
            if step == 1:
                for c in range(width):
                    ref[c, :ext, :] = place(pair_hot[:ext], contributions[c])
            else:
                add_arrived(ref, landing, 1, tile_hot, 0, nb)
            swapping.wait()
            add_arrived(ref, landing, step, one_hot, nb * step, base)
            swapping.finish()

    all_pairs(gradient_pair)

    def slot_rows(r, width):
        return slots[pl.ds(r, 2 * pairs, stride=width), :]

    contributions = []
    for a in range(3):
        speed = slot_rows(4 * ROWS + 3 + a, R1)
        plain = slot_rows((a + 1) * ROWS + 6, R1) - speed * slot_rows(6, R1)
        for b in range(3):
            bent = slot_rows((a + 1) * ROWS + b, R1) - speed * slot_rows(b, R1)
            contributions.append(slot_rows(4 * ROWS + b, R1) * plain - bent)
    give_back(sums, sums_arrived, 2, contributions)

    velocity_grad = [sums[c, :nb, :] * KERNEL_SCALE for c in range(9)]
    new_deviator, new_plastic, new_density, scaled, sound_speed = update_material(
        velocity_grad, [deviator[k] for k in range(6)], plastic[...], energy[...], density[...]
    )
    for k in range(6):
        material[k] = new_deviator[k]
        put(1 + k, scaled[k])
    material[6] = new_plastic
    material[7] = new_density
    put(0, new_density)
    put(7, sound_speed)
    put_own(stress_table)
    spread(stress_table, 4)

    all_pairs(force_pair)

    def get(r):
        return slot_rows(r, R2)

    place_of = [get(7 * ROWS + k) for k in range(3)]
    own = sym_matrix([get(8 * ROWS + 1 + k) for k in range(6)])
    other = sym_matrix([get(4 * ROWS + 1 + k) for k in range(6)])
    weight = get(6)
    drag = get(6 * ROWS + 6)
    heat = jnp.zeros_like(weight)
    contributions = []
    bent = [place_of[b] * weight - get(b) for b in range(3)]
    for a in range(3):
        speed = get(7 * ROWS + 3 + a)
        carried = get(3 + a)
        pull = get(6 * ROWS + a) - place_of[a] * drag - get(5 * ROWS + a)
        inner = place_of[a] * (get(5 * ROWS + 3 + a) - get(6 * ROWS + 3 + a))
        for b in range(3):
            pull = pull + own[a][b] * bent[b] + other[a][b] * place_of[b]
            inner = inner + own[a][b] * (place_of[b] * carried - get((a + 1) * ROWS + b))
        heat = heat + speed * pull - inner
        contributions.append(pull)
    heat = heat + get(5 * ROWS + 6) - get(6 * ROWS + 7)
    contributions.append(heat)
    give_back(pulls, pulls_arrived, 6, contributions)
    for k in range(3):
        motion[k] = pulls[k, :nb, :] * KERNEL_SCALE
    motion[3] = pulls[3, :nb, :] * (-0.5 * KERNEL_SCALE)


def body(
    sizes,
    position,
    velocity,
    particle_mass,
    density,
    deviator,
    plastic,
    energy,
    block_fill,
    pair_blocks,
    pair_count,
    slab_send,
    tile_send,
):
    n_slab, n_tile = sizes
    nb = block_fill.shape[0]
    blk = position.shape[1] // nb
    gs = slab_send.shape[1]
    pairs = pair_blocks.shape[1]
    full = nb + 4 * gs
    alive = lax.broadcasted_iota(jnp.int32, (nb, blk), 1) < block_fill[:, None]
    live_mass = jnp.where(alive, particle_mass.reshape(nb, blk), 0.0)
    first, second = pair_blocks[0], pair_blocks[1]
    live = jnp.arange(pairs, dtype=jnp.int32) < pair_count[0]
    lane = max(2 * pairs, 2 * gs)

    def line(values):
        return jnp.pad(values, (0, lane - values.shape[0]), constant_values=-1)

    ids = jnp.stack(
        [
            line(
                jnp.concatenate(
                    [
                        jnp.where(live, first, -1),
                        jnp.where(live & (first != second), second, -1),
                    ]
                )
            ),
            line(tile_send.reshape(-1)),
            line(slab_send.reshape(-1)),
        ]
    )
    smem = pl.BlockSpec(memory_space=pltpu.SMEM)
    vmem = pl.BlockSpec(memory_space=pltpu.VMEM)
    motion, material = pl.pallas_call(
        functools.partial(step_kernel, (n_slab, n_tile, nb, gs, pairs)),
        out_shape=(
            jax.ShapeDtypeStruct((4, nb, blk), F32),
            jax.ShapeDtypeStruct((8, nb, blk), F32),
        ),
        in_specs=[smem] * 3 + [vmem] * 8,
        out_specs=(vmem, vmem),
        scratch_shapes=[
            pltpu.VMEM((nb * ROWS, blk), F32),
            pltpu.VMEM((full, ROWS, blk), F32),
            pltpu.VMEM((full, ROWS, blk), F32),
            pltpu.VMEM((4, 2, gs, ROWS, blk), F32),
            pltpu.VMEM((4, 2, gs, ROWS, blk), F32),
            pltpu.VMEM((2 * pairs * R2, blk), F32),
            pltpu.VMEM((9, full, blk), F32),
            pltpu.VMEM((2, 2, 9, gs, blk), F32),
            pltpu.VMEM((4, full, blk), F32),
            pltpu.VMEM((2, 2, 4, gs, blk), F32),
            pltpu.VMEM((pairs, blk, blk), BF16),
            pltpu.VMEM((pairs, blk, blk), BF16),
            pltpu.VMEM((pairs, blk, blk), F32),
            pltpu.VMEM((2, pairs, ROWS, blk), F32),
            pltpu.SemaphoreType.DMA((8, 2)),
            pltpu.SemaphoreType.DMA((8, 2)),
        ],
        compiler_params=pltpu.CompilerParams(
            collective_id=0, has_side_effects=True, vmem_limit_bytes=40 * 1024 * 1024
        ),
    )(
        pair_blocks,
        slab_send,
        tile_send,
        ids,
        position.reshape(3, nb, blk),
        velocity.reshape(3, nb, blk),
        live_mass,
        density.reshape(nb, blk),
        deviator.reshape(6, nb, blk),
        plastic.reshape(nb, blk),
        energy.reshape(nb, blk),
    )
    return motion.reshape(4, nb * blk), material.reshape(8, nb * blk)


def solution(mesh):
    placed = (
        P(None, ("slab", "tile")),
        P(None, ("slab", "tile")),
        P(("slab", "tile")),
        P(("slab", "tile")),
        P(None, ("slab", "tile")),
        P(("slab", "tile")),
        P(("slab", "tile")),
        P(("slab", "tile")),
        P(None, ("slab", "tile")),
        P(("slab", "tile")),
        P(None, ("slab", "tile")),
        P(None, ("slab", "tile")),
    )
    return jax.shard_map(
        functools.partial(body, (mesh.shape["slab"], mesh.shape["tile"])),
        mesh=mesh,
        in_specs=placed,
        out_specs=(P(None, ("slab", "tile")), P(None, ("slab", "tile"))),
        check_vma=False,
    )
```
